32 devices in a mesh: ctx: 32 (over z, y, x, core).
Axes of the slice: x: 2, y: 2, z: 4, core: 2. Of those that a mesh axis runs over, the one named last changes fastest.
Arguments:
- queries: bfloat16 [4096, 512], P('ctx'), may hold values from -6 to 6
- keys: bfloat16 [4096, 512], P('ctx'), may hold values from -6 to 6
- values: bfloat16 [4096, 512], P('ctx'), may hold values from -6 to 6
- out_weight: bfloat16 [4096, 512], P('ctx'), may hold values from -0.25 to 0.25
- cotangent: bfloat16 [4096, 4096], P('ctx'), may hold values from -6 to 6
Outputs:
- mixed: bfloat16 [4096, 4096], P('ctx')
- query_gradient: bfloat16 [4096, 512], P('ctx')
- key_gradient: bfloat16 [4096, 512], P('ctx')
- value_gradient: bfloat16 [4096, 512], P('ctx')
- weight_grad: float32 [4096, 512], P('ctx')
The draws below stay inside these ranges and needn't reach their ends.
All inputs are finite; a program needn't handle non-finite values.
Results may differ from the reference program's by a relative error of at most 0.014.
Values may be sent and summed in bfloat16 or wider, within the bound.
A program may use at most 320 MiB of HBM per device.

```python
import jax
import jax.numpy as jnp
from jax import lax

D = 4096
HEADS = 4
HEAD = 128
HF = 512
TOK_DEV = 128
TOKENS = 4096
N_CTX = 32


def spiked(result, rng, source, target, blocks, factor):
    def block_of(position):
        return (jnp.arange(result.shape[position]) // (result.shape[position] // blocks)).reshape((-1,) + (1,) * (result.ndim - 1 - position))

    one_side = jax.random.permutation(rng, blocks)[block_of(target)]
    other_side = (block_of(target) + blocks // 2) % blocks
    return jnp.where((block_of(source) == one_side) | (block_of(source) == other_side), factor * result, result)


def level_of(stream_key, dims, split, smallest, high):
    factor_of, own = 1.0, jax.random.fold_in(stream_key, 6)
    for axis_at, blocks in split:
        heights = jnp.exp(jax.random.uniform(jax.random.fold_in(own, axis_at), (blocks,), jnp.float32, smallest / len(split), high / len(split)))
        factor_of = factor_of * jnp.repeat(heights, dims[axis_at] // blocks).reshape([-1 if axis == axis_at else 1 for axis in range(len(dims))])
    return factor_of


def bell_draw(own_key, extent, scale, most, split=(), held_as=jnp.bfloat16):
    result = scale * jax.random.normal(own_key, extent, jnp.float32)
    if split:
        result = result * level_of(own_key, extent, split, -0.22, 0.18)
    return jnp.clip(result, -most, most).astype(held_as)


def bell_draw_with(rng, dims, scale, reach, split, heavy, held_as=jnp.bfloat16):
    array = scale * jax.random.normal(rng, dims, jnp.float32)
    if split:
        array = array * level_of(rng, dims, split, -0.22, 0.18)
    return jnp.clip(spiked(array, jax.random.fold_in(rng, 3), *heavy), -reach, reach).astype(held_as)


def setup_inputs(seed: int = 0) -> dict:
    key_list = jax.random.split(jax.random.key(seed), 6)
    return {
        "queries": bell_draw(key_list[0], (TOKENS, HF), 1.0, 6.0, ((0, 32),)),
        "keys": bell_draw(key_list[1], (TOKENS, HF), 1.0, 6.0, ((0, 32),)),
        "values": bell_draw(key_list[2], (TOKENS, HF), 1.0, 6.0, ((0, 32),)),
        "out_weight": bell_draw(key_list[3], (D, HF), HF ** -0.5, 0.25, ((0, 32),)),
        "cotangent": bell_draw_with(key_list[4], (TOKENS, D), 1.0, 6.0, ((0, 32),), (0, 1, 32, 2.75)),
    }


def block_terms(items):
    head_queries, head_keys, head_values, head_gradient, prefix_key_state, state_gradient, position_scale = items
    query_wide = head_queries.astype(jnp.float32)
    key_wide = head_keys.astype(jnp.float32)
    value_wide = head_values.astype(jnp.float32)
    gradient_wide = head_gradient.astype(jnp.float32)
    prefix_key_state_wide = prefix_key_state.astype(jnp.float32)
    state_gradient_wide = state_gradient.astype(jnp.float32)
    row_index = jnp.arange(TOK_DEV, dtype=jnp.int32)
    causal = (row_index[:, None] >= row_index[None, :])[None]
    scores = jnp.einsum('shd,thd->hst', query_wide, key_wide)
    masked_scores = jnp.where(causal, scores, 0.0).astype(jnp.bfloat16).astype(jnp.float32)
    local_part = jnp.einsum('kun,nkr->ukr', masked_scores, value_wide)
    carried_over = jnp.einsum('mqw,qwi->mqi', query_wide, prefix_key_state_wide)
    attended = ((local_part + carried_over) * position_scale[:, None, None]).astype(jnp.bfloat16)
    grad_scores = jnp.einsum('shd,thd->hst', gradient_wide, value_wide)
    masked_gradient = jnp.where(causal, grad_scores, 0.0).astype(jnp.bfloat16).astype(jnp.float32)
    query_gradient = jnp.einsum('kun,nkr->ukr', masked_gradient, key_wide) + jnp.einsum('riq,ipq->rip', gradient_wide, prefix_key_state_wide)
    key_gradient = jnp.einsum('olf,loy->foy', masked_gradient, query_wide) + jnp.einsum('rwd,wed->rwe', value_wide, state_gradient_wide)
    value_gradient = jnp.einsum('olf,loy->foy', masked_scores, gradient_wide) + jnp.einsum('pyd,yda->pya', key_wide, state_gradient_wide)
    return (attended, query_gradient.astype(jnp.bfloat16), key_gradient.astype(jnp.bfloat16), value_gradient.astype(jnp.bfloat16))

def reference(queries, keys, values, out_weight, cotangent):
    positions = jnp.arange(TOKENS, dtype=jnp.int32)
    position_scale = lax.rsqrt(HEAD * (positions + 1).astype(jnp.float32))
    grad_attended = jnp.dot(cotangent, out_weight, preferred_element_type=jnp.float32)
    scaled_grad = (grad_attended * position_scale[:, None]).astype(jnp.bfloat16)
    shape_four = (N_CTX, TOK_DEV, HEADS, HEAD)
    query_blocks = queries.reshape(shape_four)
    key_blocks = keys.reshape(shape_four)
    value_blocks = values.reshape(shape_four)
    grad_blocks = scaled_grad.reshape(shape_four)
    local_keys = jnp.einsum('bthk,bthv->bhkv', key_blocks.astype(jnp.float32), value_blocks.astype(jnp.float32))
    local_grads = jnp.einsum('bthk,bthv->bhkv', query_blocks.astype(jnp.float32), grad_blocks.astype(jnp.float32))
    running_keys = jnp.cumsum(local_keys, axis=0)
    prefix_key_state = (running_keys - local_keys).astype(jnp.bfloat16)
    running_grads = jnp.cumsum(local_grads, axis=0)
    state_gradient = (running_grads[-1][None] - running_grads).astype(jnp.bfloat16)
    scale_blocks = position_scale.reshape(N_CTX, TOK_DEV)
    attended, query_gradient, key_gradient, value_gradient = lax.map(block_terms, (query_blocks, key_blocks, value_blocks, grad_blocks, prefix_key_state, state_gradient, scale_blocks))
    attended = attended.reshape(TOKENS, HF)
    mixed = lax.dot_general(attended, out_weight, (((1,), (1,)), ((), ())), preferred_element_type=jnp.float32).astype(jnp.bfloat16)
    weight_grad = lax.dot_general(cotangent, attended, (((0,), (0,)), ((), ())), preferred_element_type=jnp.float32)
    return (mixed, query_gradient.reshape(TOKENS, HF), key_gradient.reshape(TOKENS, HF), value_gradient.reshape(TOKENS, HF), weight_grad)
```

```python
import functools

import jax
import jax.numpy as jnp
from jax import lax
from jax.experimental import pallas as pl
from jax.experimental.pallas import tpu as pltpu
from jax.sharding import PartitionSpec as P

HEADS = 4
HEAD = 128
GROUP = 8
F32 = jnp.float32
BF16 = jnp.bfloat16
MESH = pl.DeviceIdType.MESH


def dot(x, y, dims):
    return lax.dot_general(x, y, (dims, ((), ())), preferred_element_type=F32)


NN = ((1,), (0,))
NT = ((1,), (1,))
TN = ((0,), (0,))


def kernel(
    planes,
    q_ref, k_ref, v_ref, w_ref, cot_ref,
    mixed_ref, dq_ref, dk_ref, dv_ref, wg_ref,
    full_w, part, from_sib, summed, from_diag, from_x, from_y, to_plane, from_plane, own_sum,
    scores, local_part, att, grad,
    piece_out, piece_in, total_out, totals, prefix_out, state,
    p1_send, p1_recv, p2_send, p2_recv, p3_send, p3_recv,
    z_send, z_recv, x_send, x_recv, y_send, y_recv, g_send, g_recv, s_send, s_recv,
    rs_send, rs_recv, rd_send, rd_recv, rx_send, rx_recv, ry_send, ry_recv, rz_send, rz_recv,
):
    tokens = q_ref.shape[0]
    rows = w_ref.shape[0]
    width = GROUP * rows
    me = lax.axis_index("ctx")
    plane = lax.div(me, GROUP)
    member = lax.rem(me, GROUP)
    core = lax.rem(member, 2)
    quad = lax.div(member, 2)
    quad_x = lax.rem(quad, 2)
    quad_y = lax.div(quad, 2)
    to_x = 1 - 2 * quad_x
    to_y = 2 - 4 * quad_y
    col_x = quad + to_x
    col_y = quad + to_y
    col_d = 3 - quad
    x_dev = me + 2 * to_x
    y_dev = me + 2 * to_y
    sib = me + 1 - 2 * core
    other = 1 - core

    def mate(r):
        return lax.rem(member + r, GROUP)

    def mate_dev(r):
        return plane * GROUP + mate(r)

    def plane_at(d):
        return lax.rem(plane + d, planes)

    def plane_before(d):
        return lax.rem(plane + planes - d, planes)

    def plane_dev(d):
        return plane_at(d) * GROUP + member

    def copy(src, dst, send, recv, device):
        return pltpu.make_async_remote_copy(
            src_ref=src, dst_ref=dst, send_sem=send, recv_sem=recv,
            device_id=(device,), device_id_type=MESH,
        )

    sent = []

    def start(c):
        c.start()
        sent.append(c)

    barrier = pltpu.get_barrier_semaphore()
    for r in range(1, GROUP):
        pl.semaphore_signal(barrier, inc=1, device_id=(mate_dev(r),), device_id_type=MESH)
    for d in range(1, planes):
        pl.semaphore_signal(barrier, inc=1, device_id=(plane_dev(d),), device_id_type=MESH)

    def head(ref, h):
        return ref[:, h * HEAD:(h + 1) * HEAD]

    def pieces(way, left, right):
        for h in range(HEADS):
            outer = dot(head(left, h), head(right, h), TN).astype(BF16)
            piece_out[way, 2 * h:2 * h + 2] = outer.reshape(2, HEAD // 2, HEAD)

    def piece_copy(way, r):
        return copy(piece_out.at[way, mate(r)], piece_in.at[way, member],
                    p1_send.at[way, r], p1_recv.at[way, r], mate_dev(r))

    def send_pieces(way):
        for r in range(1, GROUP):
            start(piece_copy(way, r))
        piece_in[way, member] = piece_out[way, member]

    def total_copy(way, d):
        return copy(total_out.at[way], totals.at[way, plane],
                    p2_send.at[way, d], p2_recv.at[way, d], plane_dev(d))

    def send_totals(way):
        for r in range(1, GROUP):
            piece_copy(way, r).wait_recv()
        total = piece_in[way, 0].astype(F32)
        for j in range(1, GROUP):
            total = total + piece_in[way, j].astype(F32)
        total_out[way] = total
        totals[way, plane] = total
        for d in range(1, planes):
            start(total_copy(way, d))

    def prefix_copy(way, r):
        return copy(prefix_out.at[way, mate(r)], state.at[way, member],
                    p3_send.at[way, r], p3_recv.at[way, r], mate_dev(r))

    def send_prefixes(way):
        for d in range(1, planes):
            total_copy(way, d).wait_recv()
        run = jnp.zeros((HEAD // 2, HEAD), F32)
        for i in range(planes):
            counts = (i < plane) if way == 0 else (i > plane)
            run = run + jnp.where(counts, totals[way, i], 0.0)
        for j in (range(GROUP) if way == 0 else range(GROUP - 1, -1, -1)):
            prefix_out[way, j] = run.astype(BF16)
            run = run + piece_in[way, j].astype(F32)
        for r in range(1, GROUP):
            start(prefix_copy(way, r))
        state[way, member] = prefix_out[way, member]

    def wait_state(way):
        for r in range(1, GROUP):
            prefix_copy(way, r).wait_recv()

    def state_of(way, h):
        return state[way, 2 * h:2 * h + 2].reshape(HEAD, HEAD)

    def z_copy(d):
        return copy(w_ref, full_w.at[plane, quad, core], z_send.at[d], z_recv.at[d], plane_dev(d))

    def block(d, col):
        return full_w.at[plane_before(d), col, core]

    def move(d, col, sems, device, first=False):
        send, recv = sems
        return copy(w_ref if first else block(d, col), block(d, col), send, recv, device)

    def x_copy(d, first=False):
        return move(d, quad, (x_send.at[d], x_recv.at[d]), x_dev, first)

    def y_copy(d, first=False):
        return move(d, quad, (y_send.at[d], y_recv.at[d]), y_dev, first)

    def diag_copy(d):
        if d % 2 == 0:
            return move(d, col_y, (g_send.at[d], g_recv.at[d]), x_dev)
        return move(d, col_x, (g_send.at[d], g_recv.at[d]), y_dev)

    def sib_copy(d, i, first=False):
        col = (quad, col_x, col_y, col_d)[i]
        return move(d, col, (s_send.at[d, i], s_recv.at[d, i]), sib, first)

    def spread(d):
        if d:
            z_copy(d).wait_recv()
        start(x_copy(d, d == 0))
        start(y_copy(d, d == 0))
        start(sib_copy(d, 0, d == 0))

    def pass_on(d):
        x_copy(d).wait_recv()
        if d % 2:
            start(diag_copy(d))
        start(sib_copy(d, 1))
        y_copy(d).wait_recv()
        if d % 2 == 0:
            start(diag_copy(d))
        start(sib_copy(d, 2))

    def pass_diag(d):
        diag_copy(d).wait_recv()
        start(sib_copy(d, 3))

    def rs_copy(d):
        return copy(part.at[d, :, other], from_sib.at[d], rs_send.at[d], rs_recv.at[d], sib)

    def reduce_1(d):
        columns = pl.ds(pl.multiple_of(plane_at(d) * width, 128), width)
        term = dot(cot_ref[:, columns], att[...], TN).astype(BF16)
        part[d] = term.reshape(4, 2, rows, term.shape[-1])
        start(rs_copy(d))

    def rd_copy(d):
        return copy(summed.at[d, col_d], from_diag.at[d], rd_send.at[d], rd_recv.at[d],
                    y_dev if d % 2 else x_dev)

    def rx_copy(d):
        return copy(summed.at[d, col_x], from_x.at[d], rx_send.at[d], rx_recv.at[d], x_dev)

    def ry_copy(d):
        return copy(summed.at[d, col_y], from_y.at[d], ry_send.at[d], ry_recv.at[d], y_dev)

    def reduce_2(d):
        rs_copy(d).wait_recv()

        def add(col):
            pair = part[d, col, core].astype(F32) + from_sib[d, col].astype(F32)
            summed[d, col] = pair.astype(BF16)

        add(col_d)
        start(rd_copy(d))
        if d % 2:
            add(col_y)
            start(ry_copy(d))
            add(col_x)
        else:
            add(col_x)
            start(rx_copy(d))
            add(col_y)

    def reduce_3(d):
        rd_copy(d).wait_recv()
        col = col_x if d % 2 else col_y
        both = summed[d, col].astype(F32) + from_diag[d].astype(F32)
        summed[d, col] = both.astype(BF16)
        start(rx_copy(d) if d % 2 else ry_copy(d))

    def rz_copy(d):
        return copy(to_plane.at[d], from_plane.at[d], rz_send.at[d], rz_recv.at[d], plane_dev(d))

    def reduce_4(d):
        rx_copy(d).wait_recv()
        ry_copy(d).wait_recv()
        pair = part[d, quad, core].astype(F32) + from_sib[d, quad].astype(F32)
        total = pair + from_x[d].astype(F32) + from_y[d].astype(F32)
        if d:
            to_plane[d] = total.astype(BF16)
            start(rz_copy(d))
        else:
            own_sum[...] = total

    def reduce_5():
        total = own_sum[...]
        for d in range(1, planes):
            rz_copy(d).wait_recv()
            total = total + from_plane[d].astype(F32)
        wg_ref[...] = total

    targets = list(range(1, planes)) + [0]

    position = me * tokens + lax.broadcasted_iota(jnp.int32, (tokens, 1), 0)
    scale = lax.rsqrt(HEAD * (position + 1).astype(F32))
    causal = lax.broadcasted_iota(jnp.int32, (tokens, tokens), 0) >= lax.broadcasted_iota(
        jnp.int32, (tokens, tokens), 1
    )

    pieces(0, k_ref, v_ref)
    pl.semaphore_wait(barrier, GROUP - 1 + planes - 1)
    send_pieces(0)
    for d in range(1, planes):
        start(z_copy(d))
    spread(0)
    full_w[plane, quad, core] = w_ref[...]
    for h in range(HEADS):
        s = jnp.where(causal, dot(head(q_ref, h), head(k_ref, h), NT), 0.0).astype(BF16)
        scores[h] = s
        local_part[h] = dot(s, head(v_ref, h), NN)
    send_totals(0)
    spread(1)
    send_prefixes(0)
    for d in range(2, planes):
        spread(d)
    wait_state(0)
    for h in range(HEADS):
        a = (local_part[h] + dot(head(q_ref, h), state_of(0, h), NN)) * scale
        att[:, h * HEAD:(h + 1) * HEAD] = a.astype(BF16)
    for d in range(planes):
        pass_on(d)
        reduce_1(targets[d])
    for d in range(planes):
        pass_diag(d)
        reduce_2(targets[d])

    grad_acc = jnp.zeros(att.shape, F32)
    for d in range(planes):
        for i in range(4):
            sib_copy(d, i).wait_recv()
    for i in range(planes):
        w = full_w[i].reshape(width, w_ref.shape[1])
        grad_acc = grad_acc + dot(cot_ref[:, i * width:(i + 1) * width], w, NN)
    grad[...] = (grad_acc * scale).astype(BF16)
    pieces(1, q_ref, grad)
    send_pieces(1)
    for d in targets:
        reduce_3(d)
    send_totals(1)
    for i in range(planes // 2):
        w = full_w[i].reshape(width, w_ref.shape[1])
        mixed_ref[:, i * width:(i + 1) * width] = dot(att[...], w, NT).astype(BF16)
    send_prefixes(1)
    for d in targets:
        reduce_4(d)
    for i in range(planes // 2, planes):
        w = full_w[i].reshape(width, w_ref.shape[1])
        mixed_ref[:, i * width:(i + 1) * width] = dot(att[...], w, NT).astype(BF16)
    wait_state(1)
    for h in range(HEADS):
        cols = slice(h * HEAD, (h + 1) * HEAD)
        q, k, v, g = head(q_ref, h), head(k_ref, h), head(v_ref, h), head(grad, h)
        gs = jnp.where(causal, dot(g, v, NT), 0.0).astype(BF16)
        dq_ref[:, cols] = (dot(gs, k, NN) + dot(g, state_of(0, h), NT)).astype(BF16)
        dk_ref[:, cols] = (dot(gs, q, TN) + dot(v, state_of(1, h), NT)).astype(BF16)
        dv_ref[:, cols] = (dot(scores[h], g, TN) + dot(k, state_of(1, h), NN)).astype(BF16)
    reduce_5()
    for c in sent:
        c.wait_send()


def body(planes, queries, keys, values, out_weight, cotangent):
    tokens, hf = queries.shape
    rows = out_weight.shape[0]
    half = HEAD // 2
    dma = pltpu.SemaphoreType.DMA
    vmem = pl.BlockSpec(memory_space=pltpu.VMEM)
    blocks = pltpu.VMEM((planes, rows, hf), BF16)
    return pl.pallas_call(
        functools.partial(kernel, planes),
        out_shape=(
            jax.ShapeDtypeStruct(cotangent.shape, BF16),
            jax.ShapeDtypeStruct(queries.shape, BF16),
            jax.ShapeDtypeStruct(queries.shape, BF16),
            jax.ShapeDtypeStruct(queries.shape, BF16),
            jax.ShapeDtypeStruct(out_weight.shape, F32),
        ),
        in_specs=[vmem] * 5,
        out_specs=(vmem,) * 5,
        scratch_shapes=[
            pltpu.VMEM((planes, 4, 2, rows, hf), BF16),
            pltpu.VMEM((planes, 4, 2, rows, hf), BF16),
            pltpu.VMEM((planes, 4, rows, hf), BF16),
            pltpu.VMEM((planes, 4, rows, hf), BF16),
            blocks, blocks, blocks, blocks, blocks,
            pltpu.VMEM((rows, hf), F32),
            pltpu.VMEM((HEADS, tokens, tokens), BF16),
            pltpu.VMEM((HEADS, tokens, HEAD), F32),
            pltpu.VMEM((tokens, hf), BF16),
            pltpu.VMEM((tokens, hf), BF16),
            pltpu.VMEM((2, GROUP, half, HEAD), BF16),
            pltpu.VMEM((2, GROUP, half, HEAD), BF16),
            pltpu.VMEM((2, half, HEAD), F32),
            pltpu.VMEM((2, planes, half, HEAD), F32),
            pltpu.VMEM((2, GROUP, half, HEAD), BF16),
            pltpu.VMEM((2, GROUP, half, HEAD), BF16),
            dma((2, GROUP)), dma((2, GROUP)),
            dma((2, planes)), dma((2, planes)),
            dma((2, GROUP)), dma((2, GROUP)),
        ] + [dma((planes,))] * 8 + [dma((planes, 4))] * 2 + [dma((planes,))] * 10,
        compiler_params=pltpu.CompilerParams(
            collective_id=0, has_side_effects=True, vmem_limit_bytes=48 * 1024 * 1024
        ),
    )(queries, keys, values, out_weight, cotangent)


def solution(mesh):
    planes = mesh.shape["ctx"] // GROUP
    spec = P("ctx", None)
    return jax.shard_map(
        functools.partial(body, planes),
        mesh=mesh,
        in_specs=(spec,) * 5,
        out_specs=(spec,) * 5,
        check_vma=False,
    )
```

```python
import functools

import jax
import jax.numpy as jnp
from jax import lax
from jax.experimental import pallas as pl
from jax.experimental.pallas import tpu as pltpu
from jax.sharding import PartitionSpec as P

HEADS = 4
HEAD = 128
GROUP = 8
F32 = jnp.float32
BF16 = jnp.bfloat16
MESH = pl.DeviceIdType.MESH


def dot(x, y, dims):
    return lax.dot_general(x, y, (dims, ((), ())), preferred_element_type=F32)


NN = ((1,), (0,))
NT = ((1,), (1,))
TN = ((0,), (0,))


def kernel(
    planes,
    q_hbm, k_hbm, v_hbm, w_ref, cot_hbm,
    mixed_ref, dq_ref, dk_ref, dv_ref, wg_ref,
    q_ref, k_ref, v_ref, cot_ref, load,
    full_w, part, from_sib, summed, from_diag, from_x, from_y, to_plane, from_plane, own_sum,
    scores, local_part, att, grad,
    piece_out, piece_in, total_out, totals, prefix_out, state,
    p1_send, p1_recv, p2_send, p2_recv, p3_send, p3_recv,
    z_send, z_recv, x_send, x_recv, y_send, y_recv, g_send, g_recv, s_send, s_recv,
    rs_send, rs_recv, rd_send, rd_recv, rx_send, rx_recv, ry_send, ry_recv, rz_send, rz_recv,
):
    tokens = q_ref.shape[0]
    rows = w_ref.shape[0]
    width = GROUP * rows
    me = lax.axis_index("ctx")
    plane = lax.div(me, GROUP)
    member = lax.rem(me, GROUP)
    core = lax.rem(member, 2)
    quad = lax.div(member, 2)
    quad_x = lax.rem(quad, 2)
    quad_y = lax.div(quad, 2)
    to_x = 1 - 2 * quad_x
    to_y = 2 - 4 * quad_y
    col_x = quad + to_x
    col_y = quad + to_y
    col_d = 3 - quad
    x_dev = me + 2 * to_x
    y_dev = me + 2 * to_y
    sib = me + 1 - 2 * core
    other = 1 - core

    def mate(r):
        return lax.rem(member + r, GROUP)

    def mate_dev(r):
        return plane * GROUP + mate(r)

    def plane_at(d):
        return lax.rem(plane + d, planes)

    def plane_before(d):
        return lax.rem(plane + planes - d, planes)

    def plane_dev(d):
        return plane_at(d) * GROUP + member

    def copy(src, dst, send, recv, device):
        return pltpu.make_async_remote_copy(
            src_ref=src, dst_ref=dst, send_sem=send, recv_sem=recv,
            device_id=(device,), device_id_type=MESH,
        )

    sent = []

    def start(c):
        c.start()
        sent.append(c)

    loads = [
        pltpu.make_async_copy(src, dst, load.at[i])
        for i, (src, dst) in enumerate((
            (k_hbm, k_ref), (v_hbm, v_ref), (q_hbm, q_ref),
            (w_ref, full_w.at[plane, quad, core]), (cot_hbm, cot_ref),
        ))
    ]
    for c in loads:
        c.start()

    barrier = pltpu.get_barrier_semaphore()
    for r in range(1, GROUP):
        pl.semaphore_signal(barrier, inc=1, device_id=(mate_dev(r),), device_id_type=MESH)
    for d in range(1, planes):
        pl.semaphore_signal(barrier, inc=1, device_id=(plane_dev(d),), device_id_type=MESH)

    def head(ref, h):
        return ref[:, h * HEAD:(h + 1) * HEAD]

    def pieces(way, left, right):
        for h in range(HEADS):
            outer = dot(head(left, h), head(right, h), TN).astype(BF16)
            piece_out[way, 2 * h:2 * h + 2] = outer.reshape(2, HEAD // 2, HEAD)

    def piece_copy(way, r):
        return copy(piece_out.at[way, mate(r)], piece_in.at[way, member],
                    p1_send.at[way, r], p1_recv.at[way, r], mate_dev(r))

    def send_pieces(way):
        for r in range(1, GROUP):
            start(piece_copy(way, r))
        piece_in[way, member] = piece_out[way, member]

    def total_copy(way, d):
        return copy(total_out.at[way], totals.at[way, plane],
                    p2_send.at[way, d], p2_recv.at[way, d], plane_dev(d))

    def send_totals(way):
        for r in range(1, GROUP):
            piece_copy(way, r).wait_recv()
        total = piece_in[way, 0].astype(F32)
        for j in range(1, GROUP):
            total = total + piece_in[way, j].astype(F32)
        total_out[way] = total
        totals[way, plane] = total
        for d in range(1, planes):
            start(total_copy(way, d))

    def prefix_copy(way, r):
        return copy(prefix_out.at[way, mate(r)], state.at[way, member],
                    p3_send.at[way, r], p3_recv.at[way, r], mate_dev(r))

    def send_prefixes(way):
        for d in range(1, planes):
            total_copy(way, d).wait_recv()
        run = jnp.zeros((HEAD // 2, HEAD), F32)
        for i in range(planes):
            counts = (i < plane) if way == 0 else (i > plane)
            run = run + jnp.where(counts, totals[way, i], 0.0)
        for j in (range(GROUP) if way == 0 else range(GROUP - 1, -1, -1)):
            prefix_out[way, j] = run.astype(BF16)
            run = run + piece_in[way, j].astype(F32)
        for r in range(1, GROUP):
            start(prefix_copy(way, r))
        state[way, member] = prefix_out[way, member]

    def wait_state(way):
        for r in range(1, GROUP):
            prefix_copy(way, r).wait_recv()

    def state_of(way, h):
        return state[way, 2 * h:2 * h + 2].reshape(HEAD, HEAD)

    def z_copy(d):
        return copy(w_ref, full_w.at[plane, quad, core], z_send.at[d], z_recv.at[d], plane_dev(d))

    def block(d, col):
        return full_w.at[plane_before(d), col, core]

    def move(d, col, sems, device, first=False):
        send, recv = sems
        return copy(w_ref if first else block(d, col), block(d, col), send, recv, device)

    def x_copy(d, first=False):
        return move(d, quad, (x_send.at[d], x_recv.at[d]), x_dev, first)

    def y_copy(d, first=False):
        return move(d, quad, (y_send.at[d], y_recv.at[d]), y_dev, first)

    def diag_copy(d):
        if d % 2 == 0:
            return move(d, col_y, (g_send.at[d], g_recv.at[d]), x_dev)
        return move(d, col_x, (g_send.at[d], g_recv.at[d]), y_dev)

    def sib_copy(d, i, first=False):
        col = (quad, col_x, col_y, col_d)[i]
        return move(d, col, (s_send.at[d, i], s_recv.at[d, i]), sib, first)

    def spread(d):
        if d:
            z_copy(d).wait_recv()
        start(x_copy(d, d == 0))
        start(y_copy(d, d == 0))
        start(sib_copy(d, 0, d == 0))

    def pass_on(d):
        x_copy(d).wait_recv()
        if d % 2:
            start(diag_copy(d))
        start(sib_copy(d, 1))
        y_copy(d).wait_recv()
        if d % 2 == 0:
            start(diag_copy(d))
        start(sib_copy(d, 2))

    def pass_diag(d):
        diag_copy(d).wait_recv()
        start(sib_copy(d, 3))

    def rs_copy(d):
        return copy(part.at[d, :, other], from_sib.at[d], rs_send.at[d], rs_recv.at[d], sib)

    def reduce_1(d):
        columns = pl.ds(pl.multiple_of(plane_at(d) * width, 128), width)
        term = dot(cot_ref[:, columns], att[...], TN).astype(BF16)
        part[d] = term.reshape(4, 2, rows, term.shape[-1])
        start(rs_copy(d))

    def rd_copy(d):
        return copy(summed.at[d, col_d], from_diag.at[d], rd_send.at[d], rd_recv.at[d],
                    y_dev if d % 2 else x_dev)

    def rx_copy(d):
        return copy(summed.at[d, col_x], from_x.at[d], rx_send.at[d], rx_recv.at[d], x_dev)

    def ry_copy(d):
        return copy(summed.at[d, col_y], from_y.at[d], ry_send.at[d], ry_recv.at[d], y_dev)

    def reduce_2(d):
        rs_copy(d).wait_recv()

        def add(col):
            pair = part[d, col, core].astype(F32) + from_sib[d, col].astype(F32)
            summed[d, col] = pair.astype(BF16)

        add(col_d)
        start(rd_copy(d))
        if d % 2:
            add(col_y)
            start(ry_copy(d))
            add(col_x)
        else:
            add(col_x)
            start(rx_copy(d))
            add(col_y)

    def reduce_3(d):
        rd_copy(d).wait_recv()
        col = col_x if d % 2 else col_y
        both = summed[d, col].astype(F32) + from_diag[d].astype(F32)
        summed[d, col] = both.astype(BF16)
        start(rx_copy(d) if d % 2 else ry_copy(d))

    def rz_copy(d):
        return copy(to_plane.at[d], from_plane.at[d], rz_send.at[d], rz_recv.at[d], plane_dev(d))

    def reduce_4(d):
        rx_copy(d).wait_recv()
        ry_copy(d).wait_recv()
        pair = part[d, quad, core].astype(F32) + from_sib[d, quad].astype(F32)
        total = pair + from_x[d].astype(F32) + from_y[d].astype(F32)
        if d:
            to_plane[d] = total.astype(BF16)
            start(rz_copy(d))
        else:
            own_sum[...] = total

    def reduce_5():
        total = own_sum[...]
        for d in range(1, planes):
            rz_copy(d).wait_recv()
            total = total + from_plane[d].astype(F32)
        wg_ref[...] = total

    targets = list(range(1, planes)) + [0]

    position = me * tokens + lax.broadcasted_iota(jnp.int32, (tokens, 1), 0)
    scale = lax.rsqrt(HEAD * (position + 1).astype(F32))
    causal = lax.broadcasted_iota(jnp.int32, (tokens, tokens), 0) >= lax.broadcasted_iota(
        jnp.int32, (tokens, tokens), 1
    )

    loads[0].wait()
    loads[1].wait()
    pieces(0, k_ref, v_ref)
    pl.semaphore_wait(barrier, GROUP - 1 + planes - 1)
    send_pieces(0)
    start(z_copy(1))
    spread(0)
    loads[2].wait()
    for h in range(HEADS):
        s = jnp.where(causal, dot(head(q_ref, h), head(k_ref, h), NT), 0.0).astype(BF16)
        scores[h] = s
        local_part[h] = dot(s, head(v_ref, h), NN)
    send_totals(0)
    for d in range(2, planes):
        start(z_copy(d))
    spread(1)
    send_prefixes(0)
    for d in range(2, planes):
        spread(d)
    pass_on(0)
    loads[3].wait()
    loads[4].wait()
    wait_state(0)
    for h in range(HEADS):
        a = (local_part[h] + dot(head(q_ref, h), state_of(0, h), NN)) * scale
        att[:, h * HEAD:(h + 1) * HEAD] = a.astype(BF16)
    for d in range(planes):
        if d:
            pass_on(d)
        reduce_1(targets[d])

    half = planes // 2
    grad_acc = jnp.zeros(att.shape, F32)
    for d in range(planes):
        pass_diag(d)
        if d % 2:
            reduce_2(targets[d // 2])
    for d in range(planes):
        for i in range(4):
            sib_copy(d, i).wait_recv()
        w = full_w[plane_before(d)].reshape(width, w_ref.shape[1])
        columns = pl.ds(pl.multiple_of(plane_before(d) * width, 128), width)
        grad_acc = grad_acc + dot(cot_ref[:, columns], w, NN)
    grad[...] = (grad_acc * scale).astype(BF16)
    pieces(1, q_ref, grad)
    send_pieces(1)
    for d in range(half):
        reduce_2(targets[half + d])
        reduce_3(targets[d])
    send_totals(1)
    for d in range(half, planes):
        reduce_3(targets[d])

    def mix(i):
        w = full_w[i].reshape(width, w_ref.shape[1])
        mixed_ref[:, i * width:(i + 1) * width] = dot(att[...], w, NT).astype(BF16)

    mix(0)
    send_prefixes(1)
    for d in range(planes):
        if d:
            mix(d)
        reduce_4(targets[d])
    wait_state(1)
    for h in range(HEADS):
        cols = slice(h * HEAD, (h + 1) * HEAD)
        q, k, v, g = head(q_ref, h), head(k_ref, h), head(v_ref, h), head(grad, h)
        gs = jnp.where(causal, dot(g, v, NT), 0.0).astype(BF16)
        dq_ref[:, cols] = (dot(gs, k, NN) + dot(g, state_of(0, h), NT)).astype(BF16)
        dk_ref[:, cols] = (dot(gs, q, TN) + dot(v, state_of(1, h), NT)).astype(BF16)
        dv_ref[:, cols] = (dot(scores[h], g, TN) + dot(k, state_of(1, h), NN)).astype(BF16)
    reduce_5()
    for c in sent:
        c.wait_send()


def place(*refs):
    sems = refs[10]
    copies = [pltpu.make_async_copy(refs[i], refs[5 + i], sems.at[i]) for i in range(5)]
    for c in copies:
        c.start()
    for c in copies:
        c.wait()


def body(planes, queries, keys, values, out_weight, cotangent):
    tokens, hf = queries.shape
    rows = out_weight.shape[0]
    half = HEAD // 2
    dma = pltpu.SemaphoreType.DMA
    vmem = pl.BlockSpec(memory_space=pltpu.VMEM)
    hbm = pl.BlockSpec(memory_space=pl.ANY)
    blocks = pltpu.VMEM((planes, rows, hf), BF16)
    results = pl.pallas_call(
        functools.partial(kernel, planes),
        out_shape=(
            jax.ShapeDtypeStruct(cotangent.shape, BF16),
            jax.ShapeDtypeStruct(queries.shape, BF16),
            jax.ShapeDtypeStruct(queries.shape, BF16),
            jax.ShapeDtypeStruct(queries.shape, BF16),
            jax.ShapeDtypeStruct(out_weight.shape, F32),
        ),
        in_specs=[hbm] * 5,
        out_specs=(vmem,) * 5,
        scratch_shapes=[
            pltpu.VMEM(queries.shape, BF16),
            pltpu.VMEM(queries.shape, BF16),
            pltpu.VMEM(queries.shape, BF16),
            pltpu.VMEM(cotangent.shape, BF16),
            dma((5,)),
            pltpu.VMEM((planes, 4, 2, rows, hf), BF16),
            pltpu.VMEM((planes, 4, 2, rows, hf), BF16),
            pltpu.VMEM((planes, 4, rows, hf), BF16),
            pltpu.VMEM((planes, 4, rows, hf), BF16),
            blocks, blocks, blocks, blocks, blocks,
            pltpu.VMEM((rows, hf), F32),
            pltpu.VMEM((HEADS, tokens, tokens), BF16),
            pltpu.VMEM((HEADS, tokens, HEAD), F32),
            pltpu.VMEM((tokens, hf), BF16),
            pltpu.VMEM((tokens, hf), BF16),
            pltpu.VMEM((2, GROUP, half, HEAD), BF16),
            pltpu.VMEM((2, GROUP, half, HEAD), BF16),
            pltpu.VMEM((2, half, HEAD), F32),
            pltpu.VMEM((2, planes, half, HEAD), F32),
            pltpu.VMEM((2, GROUP, half, HEAD), BF16),
            pltpu.VMEM((2, GROUP, half, HEAD), BF16),
            dma((2, GROUP)), dma((2, GROUP)),
            dma((2, planes)), dma((2, planes)),
            dma((2, GROUP)), dma((2, GROUP)),
        ] + [dma((planes,))] * 8 + [dma((planes, 4))] * 2 + [dma((planes,))] * 10,
        compiler_params=pltpu.CompilerParams(
            collective_id=0, has_side_effects=True, vmem_limit_bytes=60 * 1024 * 1024
        ),
    )(queries, keys, values, out_weight, cotangent)
    return pl.pallas_call(
        place,
        out_shape=[jax.ShapeDtypeStruct(r.shape, r.dtype) for r in results],
        in_specs=[hbm] * 5,
        out_specs=[hbm] * 5,
        scratch_shapes=[dma((5,))],
        compiler_params=pltpu.CompilerParams(vmem_limit_bytes=60 * 1024 * 1024),
    )(*results)


def solution(mesh):
    planes = mesh.shape["ctx"] // GROUP
    spec = P("ctx", None)
    return jax.shard_map(
        functools.partial(body, planes),
        mesh=mesh,
        in_specs=(spec,) * 5,
        out_specs=(spec,) * 5,
        check_vma=False,
    )
```

```python
import functools

import jax
import jax.numpy as jnp
from jax import lax
from jax.experimental import pallas as pl
from jax.experimental.pallas import tpu as pltpu
from jax.sharding import PartitionSpec as P

HEADS = 4
HEAD = 128
GROUP = 8
F32 = jnp.float32
BF16 = jnp.bfloat16
MESH = pl.DeviceIdType.MESH


def dot(x, y, dims):
    return lax.dot_general(x, y, (dims, ((), ())), preferred_element_type=F32)


NN = ((1,), (0,))
NT = ((1,), (1,))
TN = ((0,), (0,))


def kernel(
    planes,
    q_hbm, k_hbm, v_hbm, w_ref, cot_hbm,
    mixed_hbm, dq_hbm, dk_hbm, dv_hbm, wg_hbm,
    mixed_ref, dq_ref, dk_ref, dv_ref, wg_ref, store,
    q_ref, k_ref, v_ref, cot_ref, cot_t, load,
    full_w, part, from_sib, summed, from_diag, from_x, from_y, to_plane, from_plane, own_sum,
    scores, local_part, att, grad,
    piece_out, piece_in, total_out, totals, prefix_out, state,
    p1_send, p1_recv, p2_send, p2_recv, p3_send, p3_recv,
    z_send, z_recv, x_send, x_recv, y_send, y_recv, g_send, g_recv, s_send, s_recv,
    rs_send, rs_recv, rd_send, rd_recv, rx_send, rx_recv, ry_send, ry_recv, rz_send, rz_recv,
):
    tokens = q_ref.shape[0]
    rows = w_ref.shape[0]
    width = GROUP * rows
    me = lax.axis_index("ctx")
    plane = lax.div(me, GROUP)
    member = lax.rem(me, GROUP)
    core = lax.rem(member, 2)
    quad = lax.div(member, 2)
    quad_x = lax.rem(quad, 2)
    quad_y = lax.div(quad, 2)
    to_x = 1 - 2 * quad_x
    to_y = 2 - 4 * quad_y
    col_x = quad + to_x
    col_y = quad + to_y
    col_d = 3 - quad
    x_dev = me + 2 * to_x
    y_dev = me + 2 * to_y
    sib = me + 1 - 2 * core
    other = 1 - core

    def mate(r):
        return lax.rem(member + r, GROUP)

    def mate_dev(r):
        return plane * GROUP + mate(r)

    def plane_at(d):
        return lax.rem(plane + d, planes)

    def plane_before(d):
        return lax.rem(plane + planes - d, planes)

    def plane_dev(d):
        return plane_at(d) * GROUP + member

    def copy(src, dst, send, recv, device):
        return pltpu.make_async_remote_copy(
            src_ref=src, dst_ref=dst, send_sem=send, recv_sem=recv,
            device_id=(device,), device_id_type=MESH,
        )

    sent = []

    def start(c):
        c.start()
        sent.append(c)

    loads = [
        pltpu.make_async_copy(src, dst, load.at[i])
        for i, (src, dst) in enumerate((
            (k_hbm, k_ref), (v_hbm, v_ref), (q_hbm, q_ref),
            (w_ref, full_w.at[plane, quad, core]), (cot_hbm, cot_ref),
        ))
    ]
    for c in loads:
        c.start()

    barrier = pltpu.get_barrier_semaphore()
    for r in range(1, GROUP):
        pl.semaphore_signal(barrier, inc=1, device_id=(mate_dev(r),), device_id_type=MESH)
    for d in range(1, planes):
        pl.semaphore_signal(barrier, inc=1, device_id=(plane_dev(d),), device_id_type=MESH)

    def head(ref, h):
        return ref[:, h * HEAD:(h + 1) * HEAD]

    def pieces(way, left, right):
        for h in range(HEADS):
            outer = dot(head(left, h), head(right, h), TN).astype(BF16)
            piece_out[way, 2 * h:2 * h + 2] = outer.reshape(2, HEAD // 2, HEAD)

    def piece_copy(way, r):
        return copy(piece_out.at[way, mate(r)], piece_in.at[way, member],
                    p1_send.at[way, r], p1_recv.at[way, r], mate_dev(r))

    def send_pieces(way):
        for r in range(1, GROUP):
            start(piece_copy(way, r))
        piece_in[way, member] = piece_out[way, member]

    def total_copy(way, d):
        return copy(total_out.at[way], totals.at[way, plane],
                    p2_send.at[way, d], p2_recv.at[way, d], plane_dev(d))

    def send_totals(way):
        for r in range(1, GROUP):
            piece_copy(way, r).wait_recv()
        total = piece_in[way, 0].astype(F32)
        for j in range(1, GROUP):
            total = total + piece_in[way, j].astype(F32)
        total_out[way] = total
        totals[way, plane] = total
        for d in range(1, planes):
            start(total_copy(way, d))

    def prefix_copy(way, r):
        return copy(prefix_out.at[way, mate(r)], state.at[way, member],
                    p3_send.at[way, r], p3_recv.at[way, r], mate_dev(r))

    def send_prefixes(way):
        for d in range(1, planes):
            total_copy(way, d).wait_recv()
        run = jnp.zeros((HEAD // 2, HEAD), F32)
        for i in range(planes):
            counts = (i < plane) if way == 0 else (i > plane)
            run = run + jnp.where(counts, totals[way, i], 0.0)
        for j in (range(GROUP) if way == 0 else range(GROUP - 1, -1, -1)):
            prefix_out[way, j] = run.astype(BF16)
            run = run + piece_in[way, j].astype(F32)
        for r in range(1, GROUP):
            start(prefix_copy(way, r))
        state[way, member] = prefix_out[way, member]

    def wait_state(way):
        for r in range(1, GROUP):
            prefix_copy(way, r).wait_recv()

    def state_of(way, h):
        return state[way, 2 * h:2 * h + 2].reshape(HEAD, HEAD)

    def z_copy(d):
        return copy(w_ref, full_w.at[plane, quad, core], z_send.at[d], z_recv.at[d], plane_dev(d))

    def block(d, col):
        return full_w.at[plane_before(d), col, core]

    def move(d, col, sems, device, first=False):
        send, recv = sems
        return copy(w_ref if first else block(d, col), block(d, col), send, recv, device)

    def x_copy(d, first=False):
        return move(d, quad, (x_send.at[d], x_recv.at[d]), x_dev, first)

    def y_copy(d, first=False):
        return move(d, quad, (y_send.at[d], y_recv.at[d]), y_dev, first)

    def diag_copy(d):
        if d % 2 == 0:
            return move(d, col_y, (g_send.at[d], g_recv.at[d]), x_dev)
        return move(d, col_x, (g_send.at[d], g_recv.at[d]), y_dev)

    def sib_copy(d, i, first=False):
        col = (quad, col_x, col_y, col_d)[i]
        return move(d, col, (s_send.at[d, i], s_recv.at[d, i]), sib, first)

    def spread(d):
        if d:
            z_copy(d).wait_recv()
        start(x_copy(d, d == 0))
        start(y_copy(d, d == 0))
        start(sib_copy(d, 0, d == 0))

    def pass_on(d):
        x_copy(d).wait_recv()
        if d % 2:
            start(diag_copy(d))
        start(sib_copy(d, 1))
        y_copy(d).wait_recv()
        if d % 2 == 0:
            start(diag_copy(d))
        start(sib_copy(d, 2))

    def pass_diag(d):
        diag_copy(d).wait_recv()
        start(sib_copy(d, 3))

    def rs_copy(d):
        return copy(part.at[d, :, other], from_sib.at[d], rs_send.at[d], rs_recv.at[d], sib)

    def reduce_1(d):
        span = pl.ds(pl.multiple_of(plane_at(d) * width, 128), width)
        term = dot(cot_t[span, :], att[...], NN).astype(BF16)
        part[d] = term.reshape(4, 2, rows, term.shape[-1])
        start(rs_copy(d))

    def rd_copy(d):
        return copy(summed.at[d, col_d], from_diag.at[d], rd_send.at[d], rd_recv.at[d],
                    y_dev if d % 2 else x_dev)

    def rx_copy(d):
        return copy(summed.at[d, col_x], from_x.at[d], rx_send.at[d], rx_recv.at[d], x_dev)

    def ry_copy(d):
        return copy(summed.at[d, col_y], from_y.at[d], ry_send.at[d], ry_recv.at[d], y_dev)

    def reduce_2(d):
        rs_copy(d).wait_recv()

        def add(col):
            pair = part[d, col, core].astype(F32) + from_sib[d, col].astype(F32)
            summed[d, col] = pair.astype(BF16)

        add(col_d)
        start(rd_copy(d))
        if d % 2:
            add(col_y)
            start(ry_copy(d))
            add(col_x)
        else:
            add(col_x)
            start(rx_copy(d))
            add(col_y)

    def reduce_3(d):
        rd_copy(d).wait_recv()
        col = col_x if d % 2 else col_y
        both = summed[d, col].astype(F32) + from_diag[d].astype(F32)
        summed[d, col] = both.astype(BF16)
        start(rx_copy(d) if d % 2 else ry_copy(d))

    def rz_copy(d):
        return copy(to_plane.at[d], from_plane.at[d], rz_send.at[d], rz_recv.at[d], plane_dev(d))

    def reduce_4(d):
        rx_copy(d).wait_recv()
        ry_copy(d).wait_recv()
        pair = part[d, quad, core].astype(F32) + from_sib[d, quad].astype(F32)
        total = pair + from_x[d].astype(F32) + from_y[d].astype(F32)
        if d:
            to_plane[d] = total.astype(BF16)
            start(rz_copy(d))
        else:
            own_sum[...] = total

    def reduce_5():
        total = own_sum[...]
        for d in range(1, planes):
            rz_copy(d).wait_recv()
            total = total + from_plane[d].astype(F32)
        wg_ref[...] = total

    targets = list(range(1, planes)) + [0]

    position = me * tokens + lax.broadcasted_iota(jnp.int32, (tokens, 1), 0)
    scale = lax.rsqrt(HEAD * (position + 1).astype(F32))
    causal = lax.broadcasted_iota(jnp.int32, (tokens, tokens), 0) >= lax.broadcasted_iota(
        jnp.int32, (tokens, tokens), 1
    )

    loads[0].wait()
    loads[1].wait()
    pieces(0, k_ref, v_ref)
    pl.semaphore_wait(barrier, GROUP - 1 + planes - 1)
    send_pieces(0)
    start(z_copy(1))
    spread(0)
    loads[2].wait()
    for h in range(HEADS):
        s = jnp.where(causal, dot(head(q_ref, h), head(k_ref, h), NT), 0.0).astype(BF16)
        scores[h] = s
        local_part[h] = dot(s, head(v_ref, h), NN)
    send_totals(0)
    for d in range(2, planes):
        start(z_copy(d))
    spread(1)
    send_prefixes(0)
    pass_on(0)
    loads[3].wait()
    loads[4].wait()
    for i in range(planes):
        cot_t[i * width:(i + 1) * width, :] = cot_ref[:, i * width:(i + 1) * width].T
    spread(2)
    wait_state(0)
    for h in range(HEADS):
        a = (local_part[h] + dot(head(q_ref, h), state_of(0, h), NN)) * scale
        att[:, h * HEAD:(h + 1) * HEAD] = a.astype(BF16)
    reduce_1(targets[0])
    pass_on(1)
    reduce_1(targets[1])
    for d in range(3, planes):
        spread(d)
    for d in range(2, planes):
        reduce_1(targets[d])
        pass_on(d)

    half = planes // 2
    for d in range(planes):
        pass_diag(d)
        if d % 2:
            reduce_2(targets[d // 2])
    grad_acc = jnp.zeros(att.shape, F32)
    for d in range(planes):
        for i in range(4):
            sib_copy(d, i).wait_recv()
        w = full_w[plane_before(d)].reshape(width, w_ref.shape[1])
        columns = pl.ds(pl.multiple_of(plane_before(d) * width, 128), width)
        grad_acc = grad_acc + dot(cot_ref[:, columns], w, NN)
    grad[...] = (grad_acc * scale).astype(BF16)
    pieces(1, q_ref, grad)
    send_pieces(1)

    stores = []

    def put(i, src, dst):
        c = pltpu.make_async_copy(src, dst, store.at[i])
        c.start()
        stores.append(c)

    def mix(i):
        w = full_w[i].reshape(width, w_ref.shape[1])
        cols = pl.ds(i * width, width)
        mixed_ref[:, cols] = dot(att[...], w, NT).astype(BF16)
        put(4 + i, mixed_ref.at[:, cols], mixed_hbm.at[:, cols])

    for d in range(half):
        reduce_3(targets[d])
    for d in range(half, planes):
        reduce_2(targets[d])
    mix(0)
    send_totals(1)
    for d in range(half):
        reduce_4(targets[d])
    mix(1)
    send_prefixes(1)
    for d in range(half, planes):
        reduce_3(targets[d])
    for i in range(2, planes):
        mix(i)
    for d in range(half, planes - 1):
        reduce_4(targets[d])
    wait_state(1)
    for h in range(HEADS):
        cols = slice(h * HEAD, (h + 1) * HEAD)
        q, k, v, g = head(q_ref, h), head(k_ref, h), head(v_ref, h), head(grad, h)
        gs = jnp.where(causal, dot(g, v, NT), 0.0).astype(BF16)
        dq_ref[:, cols] = (dot(gs, k, NN) + dot(g, state_of(0, h), NT)).astype(BF16)
        dk_ref[:, cols] = (dot(gs, q, TN) + dot(v, state_of(1, h), NT)).astype(BF16)
        dv_ref[:, cols] = (dot(scores[h], g, TN) + dot(k, state_of(1, h), NN)).astype(BF16)
    put(0, dq_ref, dq_hbm)
    put(1, dk_ref, dk_hbm)
    put(2, dv_ref, dv_hbm)
    reduce_4(0)
    reduce_5()
    put(3, wg_ref, wg_hbm)
    for c in sent:
        c.wait_send()
    for c in stores:
        c.wait()


def place(*refs):
    load, store = refs[15:]
    loads = [pltpu.make_async_copy(refs[i], refs[10 + i], load.at[i]) for i in range(5)]
    stores = [pltpu.make_async_copy(refs[10 + i], refs[5 + i], store.at[i]) for i in range(5)]
    for c in loads:
        c.start()
    for i in range(5):
        loads[i].wait()
        stores[i].start()
    for c in stores:
        c.wait()


def body(planes, queries, keys, values, out_weight, cotangent):
    tokens, hf = queries.shape
    rows = out_weight.shape[0]
    half = HEAD // 2
    dma = pltpu.SemaphoreType.DMA
    hbm = pl.BlockSpec(memory_space=pl.ANY)
    blocks = pltpu.VMEM((planes, rows, hf), BF16)
    results = pl.pallas_call(
        functools.partial(kernel, planes),
        out_shape=(
            jax.ShapeDtypeStruct(cotangent.shape, BF16),
            jax.ShapeDtypeStruct(queries.shape, BF16),
            jax.ShapeDtypeStruct(queries.shape, BF16),
            jax.ShapeDtypeStruct(queries.shape, BF16),
            jax.ShapeDtypeStruct(out_weight.shape, F32),
        ),
        in_specs=[hbm] * 5,
        out_specs=(hbm,) * 5,
        scratch_shapes=[
            pltpu.VMEM(cotangent.shape, BF16),
            pltpu.VMEM(queries.shape, BF16),
            pltpu.VMEM(queries.shape, BF16),
            pltpu.VMEM(queries.shape, BF16),
            pltpu.VMEM(out_weight.shape, F32),
            dma((4 + planes,)),
            pltpu.VMEM(queries.shape, BF16),
            pltpu.VMEM(queries.shape, BF16),
            pltpu.VMEM(queries.shape, BF16),
            pltpu.VMEM(cotangent.shape, BF16),
            pltpu.VMEM(cotangent.shape[::-1], BF16),
            dma((5,)),
            pltpu.VMEM((planes, 4, 2, rows, hf), BF16),
            pltpu.VMEM((planes, 4, 2, rows, hf), BF16),
            pltpu.VMEM((planes, 4, rows, hf), BF16),
            pltpu.VMEM((planes, 4, rows, hf), BF16),
            blocks, blocks, blocks, blocks, blocks,
            pltpu.VMEM((rows, hf), F32),
            pltpu.VMEM((HEADS, tokens, tokens), BF16),
            pltpu.VMEM((HEADS, tokens, HEAD), F32),
            pltpu.VMEM((tokens, hf), BF16),
            pltpu.VMEM((tokens, hf), BF16),
            pltpu.VMEM((2, GROUP, half, HEAD), BF16),
            pltpu.VMEM((2, GROUP, half, HEAD), BF16),
            pltpu.VMEM((2, half, HEAD), F32),
            pltpu.VMEM((2, planes, half, HEAD), F32),
            pltpu.VMEM((2, GROUP, half, HEAD), BF16),
            pltpu.VMEM((2, GROUP, half, HEAD), BF16),
            dma((2, GROUP)), dma((2, GROUP)),
            dma((2, planes)), dma((2, planes)),
            dma((2, GROUP)), dma((2, GROUP)),
        ] + [dma((planes,))] * 8 + [dma((planes, 4))] * 2 + [dma((planes,))] * 10,
        compiler_params=pltpu.CompilerParams(
            collective_id=0, has_side_effects=True, vmem_limit_bytes=60 * 1024 * 1024
        ),
    )(queries, keys, values, out_weight, cotangent)
    return pl.pallas_call(
        place,
        out_shape=[jax.ShapeDtypeStruct(r.shape, r.dtype) for r in results],
        in_specs=[hbm] * 5,
        out_specs=[hbm] * 5,
        scratch_shapes=[pltpu.VMEM(r.shape, r.dtype) for r in results] + [dma((5,))] * 2,
        compiler_params=pltpu.CompilerParams(vmem_limit_bytes=60 * 1024 * 1024),
    )(*results)


def solution(mesh):
    planes = mesh.shape["ctx"] // GROUP
    spec = P("ctx", None)
    return jax.shard_map(
        functools.partial(body, planes),
        mesh=mesh,
        in_specs=(spec,) * 5,
        out_specs=(spec,) * 5,
        check_vma=False,
    )
```

```python
import functools

import jax
import jax.numpy as jnp
from jax import lax
from jax.experimental import pallas as pl
from jax.experimental.pallas import tpu as pltpu
from jax.sharding import PartitionSpec as P

HEADS = 4
HEAD = 128
GROUP = 8
F32 = jnp.float32
BF16 = jnp.bfloat16
MESH = pl.DeviceIdType.MESH


def dot(x, y, dims):
    return lax.dot_general(x, y, (dims, ((), ())), preferred_element_type=F32)


NN = ((1,), (0,))
NT = ((1,), (1,))
TN = ((0,), (0,))


def kernel(
    planes,
    q_hbm, k_hbm, v_hbm, w_ref, cot_hbm,
    mixed_hbm, dq_hbm, dk_hbm, dv_hbm, wg_hbm,
    mixed_ref, dq_ref, dk_ref, dv_ref, wg_ref, store,
    q_ref, k_ref, v_ref, cot_ref, cot_t, load,
    full_w, cot_in, att_in, to_plane, from_plane, own_sum,
    scores, local_part, att, grad,
    piece_out, piece_in, total_out, totals, prefix_out, state,
    p1_send, p1_recv, p2_send, p2_recv, p3_send, p3_recv,
    z_send, z_recv, x_send, x_recv, y_send, y_recv, g_send, g_recv, s_send, s_recv,
    rz_send, rz_recv, c_send, c_recv, a_send, a_recv,
):
    tokens = q_ref.shape[0]
    rows = w_ref.shape[0]
    width = GROUP * rows
    me = lax.axis_index("ctx")
    plane = lax.div(me, GROUP)
    member = lax.rem(me, GROUP)
    core = lax.rem(member, 2)
    quad = lax.div(member, 2)
    quad_x = lax.rem(quad, 2)
    quad_y = lax.div(quad, 2)
    to_x = 1 - 2 * quad_x
    to_y = 2 - 4 * quad_y
    col_x = quad + to_x
    col_y = quad + to_y
    col_d = 3 - quad
    x_dev = me + 2 * to_x
    y_dev = me + 2 * to_y
    sib = me + 1 - 2 * core
    other = 1 - core

    def mate(r):
        return lax.rem(member + r, GROUP)

    def mate_dev(r):
        return plane * GROUP + mate(r)

    def plane_at(d):
        return lax.rem(plane + d, planes)

    def plane_before(d):
        return lax.rem(plane + planes - d, planes)

    def plane_dev(d):
        return plane_at(d) * GROUP + member

    def copy(src, dst, send, recv, device):
        return pltpu.make_async_remote_copy(
            src_ref=src, dst_ref=dst, send_sem=send, recv_sem=recv,
            device_id=(device,), device_id_type=MESH,
        )

    sent = []

    def start(c):
        c.start()
        sent.append(c)

    loads = [
        pltpu.make_async_copy(src, dst, load.at[i])
        for i, (src, dst) in enumerate((
            (k_hbm, k_ref), (v_hbm, v_ref), (q_hbm, q_ref),
            (w_ref, full_w.at[plane, quad, core]), (cot_hbm, cot_ref),
        ))
    ]
    for c in loads:
        c.start()

    barrier = pltpu.get_barrier_semaphore()
    for r in range(1, GROUP):
        pl.semaphore_signal(barrier, inc=1, device_id=(mate_dev(r),), device_id_type=MESH)
    for d in range(1, planes):
        pl.semaphore_signal(barrier, inc=1, device_id=(plane_dev(d),), device_id_type=MESH)

    def head(ref, h):
        return ref[:, h * HEAD:(h + 1) * HEAD]

    def pieces(way, left, right):
        for h in range(HEADS):
            outer = dot(head(left, h), head(right, h), TN).astype(BF16)
            piece_out[way, 2 * h:2 * h + 2] = outer.reshape(2, HEAD // 2, HEAD)

    def piece_copy(way, r):
        return copy(piece_out.at[way, mate(r)], piece_in.at[way, member],
                    p1_send.at[way, r], p1_recv.at[way, r], mate_dev(r))

    def send_pieces(way):
        for r in range(1, GROUP):
            start(piece_copy(way, r))
        piece_in[way, member] = piece_out[way, member]

    def total_copy(way, d):
        return copy(total_out.at[way], totals.at[way, plane],
                    p2_send.at[way, d], p2_recv.at[way, d], plane_dev(d))

    def send_totals(way):
        for r in range(1, GROUP):
            piece_copy(way, r).wait_recv()
        total = piece_in[way, 0].astype(F32)
        for j in range(1, GROUP):
            total = total + piece_in[way, j].astype(F32)
        total_out[way] = total
        totals[way, plane] = total
        for d in range(1, planes):
            start(total_copy(way, d))

    def prefix_copy(way, r):
        return copy(prefix_out.at[way, mate(r)], state.at[way, member],
                    p3_send.at[way, r], p3_recv.at[way, r], mate_dev(r))

    def send_prefixes(way):
        for d in range(1, planes):
            total_copy(way, d).wait_recv()
        run = jnp.zeros((HEAD // 2, HEAD), F32)
        for i in range(planes):
            counts = (i < plane) if way == 0 else (i > plane)
            run = run + jnp.where(counts, totals[way, i], 0.0)
        for j in (range(GROUP) if way == 0 else range(GROUP - 1, -1, -1)):
            prefix_out[way, j] = run.astype(BF16)
            run = run + piece_in[way, j].astype(F32)
        for r in range(1, GROUP):
            start(prefix_copy(way, r))
        state[way, member] = prefix_out[way, member]

    def wait_state(way):
        for r in range(1, GROUP):
            prefix_copy(way, r).wait_recv()

    def state_of(way, h):
        return state[way, 2 * h:2 * h + 2].reshape(HEAD, HEAD)

    def z_copy(d):
        return copy(w_ref, full_w.at[plane, quad, core], z_send.at[d], z_recv.at[d], plane_dev(d))

    def block(d, col):
        return full_w.at[plane_before(d), col, core]

    def move(d, col, sems, device, first=False):
        send, recv = sems
        return copy(w_ref if first else block(d, col), block(d, col), send, recv, device)

    def x_copy(d, first=False):
        return move(d, quad, (x_send.at[d], x_recv.at[d]), x_dev, first)

    def y_copy(d, first=False):
        return move(d, quad, (y_send.at[d], y_recv.at[d]), y_dev, first)

    def diag_copy(d):
        if d % 2 == 0:
            return move(d, col_y, (g_send.at[d], g_recv.at[d]), x_dev)
        return move(d, col_x, (g_send.at[d], g_recv.at[d]), y_dev)

    def sib_copy(d, i, first=False):
        col = (quad, col_x, col_y, col_d)[i]
        return move(d, col, (s_send.at[d, i], s_recv.at[d, i]), sib, first)

    def spread(d):
        if d:
            z_copy(d).wait_recv()
        start(x_copy(d, d == 0))
        start(y_copy(d, d == 0))
        start(sib_copy(d, 0, d == 0))

    def pass_on(d):
        x_copy(d).wait_recv()
        if d % 2:
            start(diag_copy(d))
        start(sib_copy(d, 1))
        y_copy(d).wait_recv()
        if d % 2 == 0:
            start(diag_copy(d))
        start(sib_copy(d, 2))

    def pass_diag(d):
        diag_copy(d).wait_recv()
        start(sib_copy(d, 3))

    def cot_copy(r):
        return copy(cot_t.at[:, mate(r)], cot_in.at[member], c_send.at[r], c_recv.at[r], mate_dev(r))

    def att_copy(i):
        half = tokens // 2
        col, rows_of, device = (
            (quad, None, x_dev), (quad, None, y_dev), (quad, None, sib), (col_x, None, sib),
            (col_x, pl.ds(half, half), y_dev), (col_y, None, sib), (col_y, pl.ds(0, half), x_dev),
            (col_d, None, sib),
        )[i]
        ref = att_in.at[col, core] if rows_of is None else att_in.at[col, core, rows_of]
        return copy(ref, ref, a_send.at[i], a_recv.at[i], device)

    def rz_copy(d):
        return copy(to_plane.at[d], from_plane.at[d], rz_send.at[d], rz_recv.at[d], plane_dev(d))

    def reduce_plane():
        for r in range(1, GROUP):
            cot_copy(r).wait_recv()
        for i in (2, 3, 5, 7):
            att_copy(i).wait_recv()
        tall = jnp.concatenate([
            jnp.concatenate([cot_in[j, plane_at(d)] for j in range(GROUP)], axis=1) for d in targets
        ], axis=0)
        total = dot(tall, att_in[...].reshape(GROUP * tokens, HEADS * HEAD), NN)
        for i, d in enumerate(targets):
            block_sum = total[i * rows:(i + 1) * rows]
            if d:
                to_plane[d] = block_sum.astype(BF16)
                start(rz_copy(d))
            else:
                own_sum[...] = block_sum

    def reduce_5():
        total = own_sum[...]
        for d in range(1, planes):
            rz_copy(d).wait_recv()
            total = total + from_plane[d].astype(F32)
        wg_ref[...] = total

    targets = list(range(1, planes)) + [0]

    position = me * tokens + lax.broadcasted_iota(jnp.int32, (tokens, 1), 0)
    scale = lax.rsqrt(HEAD * (position + 1).astype(F32))
    causal = lax.broadcasted_iota(jnp.int32, (tokens, tokens), 0) >= lax.broadcasted_iota(
        jnp.int32, (tokens, tokens), 1
    )

    loads[0].wait()
    loads[1].wait()
    pieces(0, k_ref, v_ref)
    pl.semaphore_wait(barrier, GROUP - 1 + planes - 1)
    send_pieces(0)
    start(z_copy(1))
    spread(0)
    loads[2].wait()
    for h in range(HEADS):
        s = jnp.where(causal, dot(head(q_ref, h), head(k_ref, h), NT), 0.0).astype(BF16)
        scores[h] = s
        local_part[h] = dot(s, head(v_ref, h), NN)
    send_totals(0)
    for d in range(2, planes):
        start(z_copy(d))
    loads[4].wait()
    for i in range(planes):
        cot_t[i] = cot_ref[:, i * width:(i + 1) * width].T.reshape(GROUP, rows, tokens)
    for r in range(1, 4):
        start(cot_copy(r))
    spread(1)
    send_prefixes(0)
    for r in range(4, GROUP):
        start(cot_copy(r))
    cot_in[member] = cot_t[:, member]
    pass_on(0)
    spread(2)
    loads[3].wait()
    wait_state(0)
    for h in range(HEADS):
        a = (local_part[h] + dot(head(q_ref, h), state_of(0, h), NN)) * scale
        att[:, h * HEAD:(h + 1) * HEAD] = a.astype(BF16)
    att_in[quad, core] = att[...]
    for i in range(3):
        start(att_copy(i))
    pass_on(1)
    for d in range(3, planes):
        spread(d)
    att_copy(0).wait_recv()
    start(att_copy(4))
    start(att_copy(3))
    att_copy(1).wait_recv()
    start(att_copy(6))
    start(att_copy(5))
    for d in range(2, planes):
        pass_on(d)
    att_copy(4).wait_recv()
    att_copy(6).wait_recv()
    start(att_copy(7))
    for d in range(planes):
        pass_diag(d)
    reduce_plane()
    grad_acc = jnp.zeros(att.shape, F32)
    for d in range(planes):
        for i in range(4):
            sib_copy(d, i).wait_recv()
        w = full_w[plane_before(d)].reshape(width, w_ref.shape[1])
        columns = pl.ds(pl.multiple_of(plane_before(d) * width, 128), width)
        grad_acc = grad_acc + dot(cot_ref[:, columns], w, NN)
    grad[...] = (grad_acc * scale).astype(BF16)
    pieces(1, q_ref, grad)
    send_pieces(1)

    stores = []

    def put(i, src, dst):
        c = pltpu.make_async_copy(src, dst, store.at[i])
        c.start()
        stores.append(c)

    def mix(i):
        w = full_w[i].reshape(width, w_ref.shape[1])
        cols = pl.ds(i * width, width)
        mixed_ref[:, cols] = dot(att[...], w, NT).astype(BF16)
        put(4 + i, mixed_ref.at[:, cols], mixed_hbm.at[:, cols])

    half = planes // 2
    for i in range(half):
        mix(i)
    send_totals(1)
    mix(half)
    send_prefixes(1)
    for i in range(half + 1, planes):
        mix(i)
    wait_state(1)
    for h in range(HEADS):
        cols = slice(h * HEAD, (h + 1) * HEAD)
        q, k, v, g = head(q_ref, h), head(k_ref, h), head(v_ref, h), head(grad, h)
        gs = jnp.where(causal, dot(g, v, NT), 0.0).astype(BF16)
        dq_ref[:, cols] = (dot(gs, k, NN) + dot(g, state_of(0, h), NT)).astype(BF16)
        dk_ref[:, cols] = (dot(gs, q, TN) + dot(v, state_of(1, h), NT)).astype(BF16)
        dv_ref[:, cols] = (dot(scores[h], g, TN) + dot(k, state_of(1, h), NN)).astype(BF16)
    put(0, dq_ref, dq_hbm)
    put(1, dk_ref, dk_hbm)
    put(2, dv_ref, dv_hbm)
    reduce_5()
    put(3, wg_ref, wg_hbm)
    for c in sent:
        c.wait_send()
    for c in stores:
        c.wait()


def place(*refs):
    load, store = refs[15:]
    loads = [pltpu.make_async_copy(refs[i], refs[10 + i], load.at[i]) for i in range(5)]
    stores = [pltpu.make_async_copy(refs[10 + i], refs[5 + i], store.at[i]) for i in range(5)]
    for c in loads:
        c.start()
    for i in range(5):
        loads[i].wait()
        stores[i].start()
    for c in stores:
        c.wait()


def body(planes, queries, keys, values, out_weight, cotangent):
    tokens, hf = queries.shape
    rows = out_weight.shape[0]
    half = HEAD // 2
    dma = pltpu.SemaphoreType.DMA
    hbm = pl.BlockSpec(memory_space=pl.ANY)
    blocks = pltpu.VMEM((planes, rows, hf), BF16)
    results = pl.pallas_call(
        functools.partial(kernel, planes),
        out_shape=(
            jax.ShapeDtypeStruct(cotangent.shape, BF16),
            jax.ShapeDtypeStruct(queries.shape, BF16),
            jax.ShapeDtypeStruct(queries.shape, BF16),
            jax.ShapeDtypeStruct(queries.shape, BF16),
            jax.ShapeDtypeStruct(out_weight.shape, F32),
        ),
        in_specs=[hbm] * 5,
        out_specs=(hbm,) * 5,
        scratch_shapes=[
            pltpu.VMEM(cotangent.shape, BF16),
            pltpu.VMEM(queries.shape, BF16),
            pltpu.VMEM(queries.shape, BF16),
            pltpu.VMEM(queries.shape, BF16),
            pltpu.VMEM(out_weight.shape, F32),
            dma((4 + planes,)),
            pltpu.VMEM(queries.shape, BF16),
            pltpu.VMEM(queries.shape, BF16),
            pltpu.VMEM(queries.shape, BF16),
            pltpu.VMEM(cotangent.shape, BF16),
            pltpu.VMEM((planes, GROUP, rows, tokens), BF16),
            dma((5,)),
            pltpu.VMEM((planes, 4, 2, rows, hf), BF16),
            pltpu.VMEM((GROUP, planes, rows, tokens), BF16),
            pltpu.VMEM((4, 2, tokens, hf), BF16),
            blocks, blocks,
            pltpu.VMEM((rows, hf), F32),
            pltpu.VMEM((HEADS, tokens, tokens), BF16),
            pltpu.VMEM((HEADS, tokens, HEAD), F32),
            pltpu.VMEM((tokens, hf), BF16),
            pltpu.VMEM((tokens, hf), BF16),
            pltpu.VMEM((2, GROUP, half, HEAD), BF16),
            pltpu.VMEM((2, GROUP, half, HEAD), BF16),
            pltpu.VMEM((2, half, HEAD), F32),
            pltpu.VMEM((2, planes, half, HEAD), F32),
            pltpu.VMEM((2, GROUP, half, HEAD), BF16),
            pltpu.VMEM((2, GROUP, half, HEAD), BF16),
            dma((2, GROUP)), dma((2, GROUP)),
            dma((2, planes)), dma((2, planes)),
            dma((2, GROUP)), dma((2, GROUP)),
        ] + [dma((planes,))] * 8 + [dma((planes, 4))] * 2 + [dma((planes,))] * 2 + [dma((GROUP,))] * 4,
        compiler_params=pltpu.CompilerParams(
            collective_id=0, has_side_effects=True, vmem_limit_bytes=60 * 1024 * 1024
        ),
    )(queries, keys, values, out_weight, cotangent)
    return pl.pallas_call(
        place,
        out_shape=[jax.ShapeDtypeStruct(r.shape, r.dtype) for r in results],
        in_specs=[hbm] * 5,
        out_specs=[hbm] * 5,
        scratch_shapes=[pltpu.VMEM(r.shape, r.dtype) for r in results] + [dma((5,))] * 2,
        compiler_params=pltpu.CompilerParams(vmem_limit_bytes=60 * 1024 * 1024),
    )(*results)


def solution(mesh):
    planes = mesh.shape["ctx"] // GROUP
    spec = P("ctx", None)
    return jax.shard_map(
        functools.partial(body, planes),
        mesh=mesh,
        in_specs=(spec,) * 5,
        out_specs=(spec,) * 5,
        check_vma=False,
    )
```

```python
import functools

import jax
import jax.numpy as jnp
from jax import lax
from jax.experimental import pallas as pl
from jax.experimental.pallas import tpu as pltpu
from jax.sharding import PartitionSpec as P

HEADS = 4
HEAD = 128
GROUP = 8
F32 = jnp.float32
BF16 = jnp.bfloat16
MESH = pl.DeviceIdType.MESH


def dot(x, y, dims):
    return lax.dot_general(x, y, (dims, ((), ())), preferred_element_type=F32)


NN = ((1,), (0,))
NT = ((1,), (1,))
TN = ((0,), (0,))


def kernel(
    planes,
    q_hbm, k_hbm, v_hbm, w_ref, cot_hbm,
    mixed_hbm, dq_hbm, dk_hbm, dv_hbm, wg_hbm,
    mixed_ref, dq_ref, dk_ref, dv_ref, wg_ref, store,
    q_ref, k_ref, v_ref, cot_ref, cot_t, load,
    cot_sib, cot_sel, att_pair, att_sib, grad_sib, grad_in, dk_part, dv_part,
    full_w, summed, from_diag, from_x, from_y, to_plane, from_plane, own_sum,
    scores, local_part, att, grad,
    piece_out, piece_in, total_out, totals, prefix_out, state,
    p1_send, p1_recv, p2_send, p2_recv, p3_send, p3_recv,
    z_send, z_recv, x_send, x_recv, y_send, y_recv, g_send, g_recv, s_send, s_recv,
    e_send, e_recv, rd_send, rd_recv, rx_send, rx_recv, ry_send, ry_recv, rz_send, rz_recv,
):
    tokens = q_ref.shape[0]
    rows = w_ref.shape[0]
    width = GROUP * rows
    me = lax.axis_index("ctx")
    plane = lax.div(me, GROUP)
    member = lax.rem(me, GROUP)
    core = lax.rem(member, 2)
    quad = lax.div(member, 2)
    quad_x = lax.rem(quad, 2)
    quad_y = lax.div(quad, 2)
    to_x = 1 - 2 * quad_x
    to_y = 2 - 4 * quad_y
    col_x = quad + to_x
    col_y = quad + to_y
    col_d = 3 - quad
    x_dev = me + 2 * to_x
    y_dev = me + 2 * to_y
    sib = me + 1 - 2 * core
    other = 1 - core

    def mate(r):
        return lax.rem(member + r, GROUP)

    def mate_dev(r):
        return plane * GROUP + mate(r)

    def plane_at(d):
        return lax.rem(plane + d, planes)

    def plane_before(d):
        return lax.rem(plane + planes - d, planes)

    def plane_dev(d):
        return plane_at(d) * GROUP + member

    def copy(src, dst, send, recv, device):
        return pltpu.make_async_remote_copy(
            src_ref=src, dst_ref=dst, send_sem=send, recv_sem=recv,
            device_id=(device,), device_id_type=MESH,
        )

    sent = []

    def start(c):
        c.start()
        sent.append(c)

    loads = [
        pltpu.make_async_copy(src, dst, load.at[i])
        for i, (src, dst) in enumerate((
            (k_hbm, k_ref), (v_hbm, v_ref), (q_hbm, q_ref),
            (w_ref, full_w.at[plane, quad, core]), (cot_hbm, cot_ref),
        ))
    ]
    for c in loads:
        c.start()

    barrier = pltpu.get_barrier_semaphore()
    for r in range(1, GROUP):
        pl.semaphore_signal(barrier, inc=1, device_id=(mate_dev(r),), device_id_type=MESH)
    for d in range(1, planes):
        pl.semaphore_signal(barrier, inc=1, device_id=(plane_dev(d),), device_id_type=MESH)

    def head(ref, h):
        return ref[:, h * HEAD:(h + 1) * HEAD]

    def pieces(way, left, right):
        for h in range(HEADS):
            outer = dot(head(left, h), head(right, h), TN).astype(BF16)
            piece_out[way, 2 * h:2 * h + 2] = outer.reshape(2, HEAD // 2, HEAD)

    def piece_copy(way, r):
        return copy(piece_out.at[way, mate(r)], piece_in.at[way, member],
                    p1_send.at[way, r], p1_recv.at[way, r], mate_dev(r))

    def send_pieces(way):
        for r in range(1, GROUP):
            start(piece_copy(way, r))
        piece_in[way, member] = piece_out[way, member]

    def total_copy(way, d):
        return copy(total_out.at[way], totals.at[way, plane],
                    p2_send.at[way, d], p2_recv.at[way, d], plane_dev(d))

    def send_totals(way):
        for r in range(1, GROUP):
            piece_copy(way, r).wait_recv()
        total = piece_in[way, 0].astype(F32)
        for j in range(1, GROUP):
            total = total + piece_in[way, j].astype(F32)
        total_out[way] = total
        totals[way, plane] = total
        for d in range(1, planes):
            start(total_copy(way, d))

    def prefix_copy(way, r):
        return copy(prefix_out.at[way, mate(r)], state.at[way, member],
                    p3_send.at[way, r], p3_recv.at[way, r], mate_dev(r))

    def send_prefixes(way):
        for d in range(1, planes):
            total_copy(way, d).wait_recv()
        run = jnp.zeros((HEAD // 2, HEAD), F32)
        for i in range(planes):
            counts = (i < plane) if way == 0 else (i > plane)
            run = run + jnp.where(counts, totals[way, i], 0.0)
        for j in (range(GROUP) if way == 0 else range(GROUP - 1, -1, -1)):
            prefix_out[way, j] = run.astype(BF16)
            run = run + piece_in[way, j].astype(F32)
        for r in range(1, GROUP):
            start(prefix_copy(way, r))
        state[way, member] = prefix_out[way, member]

    def wait_state(way):
        for r in range(1, GROUP):
            prefix_copy(way, r).wait_recv()

    def state_of(way, h):
        return state[way, 2 * h:2 * h + 2].reshape(HEAD, HEAD)

    def z_copy(d):
        return copy(w_ref, full_w.at[plane, quad, core], z_send.at[d], z_recv.at[d], plane_dev(d))

    def block(d, col):
        return full_w.at[plane_before(d), col, core]

    def move(d, col, sems, device, first=False):
        send, recv = sems
        return copy(w_ref if first else block(d, col), block(d, col), send, recv, device)

    def x_copy(d, first=False):
        return move(d, quad, (x_send.at[d], x_recv.at[d]), x_dev, first)

    def y_copy(d, first=False):
        return move(d, quad, (y_send.at[d], y_recv.at[d]), y_dev, first)

    def diag_copy(d):
        if d % 2 == 0:
            return move(d, col_y, (g_send.at[d], g_recv.at[d]), x_dev)
        return move(d, col_x, (g_send.at[d], g_recv.at[d]), y_dev)

    def sib_copy(d, i, first=False):
        col = (quad, col_x, col_y, col_d)[i]
        return move(d, col, (s_send.at[d, i], s_recv.at[d, i]), sib, first)

    def spread(d):
        if d:
            z_copy(d).wait_recv()
        start(x_copy(d, d == 0))
        start(y_copy(d, d == 0))
        start(sib_copy(d, 0, d == 0))

    def pass_on(d):
        x_copy(d).wait_recv()
        if d % 2:
            start(diag_copy(d))
        start(sib_copy(d, 1))
        y_copy(d).wait_recv()
        if d % 2 == 0:
            start(diag_copy(d))
        start(sib_copy(d, 2))

    def pass_diag(d):
        diag_copy(d).wait_recv()
        start(sib_copy(d, 3))

    exchanges = [
        copy(src, dst, e_send.at[i], e_recv.at[i], sib)
        for i, (src, dst) in enumerate((
            (cot_t.at[:, :, other], cot_sib), (att, att_sib), (grad_sib, grad_in),
        ))
    ]

    def rd_copy(d):
        return copy(summed.at[d, col_d], from_diag.at[d], rd_send.at[d], rd_recv.at[d],
                    y_dev if d % 2 else x_dev)

    def rx_copy(d):
        return copy(summed.at[d, col_x], from_x.at[d], rx_send.at[d], rx_recv.at[d], x_dev)

    def ry_copy(d):
        return copy(summed.at[d, col_y], from_y.at[d], ry_send.at[d], ry_recv.at[d], y_dev)

    def reduce_2(d):
        a = plane_at(d)
        tall = jnp.concatenate([cot_t[a, :, core], cot_sib[a]], axis=-1)
        term = dot(tall.reshape(4 * rows, 2 * tokens), att_pair[...], NN).astype(BF16)
        summed[d] = term.reshape(4, rows, HEADS * HEAD)
        start(rd_copy(d))
        start(ry_copy(d) if d % 2 else rx_copy(d))

    def reduce_3(d):
        rd_copy(d).wait_recv()
        col = col_x if d % 2 else col_y
        both = summed[d, col].astype(F32) + from_diag[d].astype(F32)
        summed[d, col] = both.astype(BF16)
        start(rx_copy(d) if d % 2 else ry_copy(d))

    def rz_copy(d):
        return copy(to_plane.at[d], from_plane.at[d], rz_send.at[d], rz_recv.at[d], plane_dev(d))

    def reduce_4(d):
        rx_copy(d).wait_recv()
        ry_copy(d).wait_recv()
        total = summed[d, quad].astype(F32) + from_x[d].astype(F32) + from_y[d].astype(F32)
        if d:
            to_plane[d] = total.astype(BF16)
            start(rz_copy(d))
        else:
            own_sum[...] = total

    def reduce_5():
        total = own_sum[...]
        for d in range(1, planes):
            rz_copy(d).wait_recv()
            total = total + from_plane[d].astype(F32)
        wg_ref[...] = total

    targets = list(range(1, planes)) + [0]

    position = me * tokens + lax.broadcasted_iota(jnp.int32, (tokens, 1), 0)
    scale = lax.rsqrt(HEAD * (position + 1).astype(F32))
    causal = lax.broadcasted_iota(jnp.int32, (tokens, tokens), 0) >= lax.broadcasted_iota(
        jnp.int32, (tokens, tokens), 1
    )

    loads[0].wait()
    loads[1].wait()
    pieces(0, k_ref, v_ref)
    pl.semaphore_wait(barrier, GROUP - 1 + planes - 1)
    send_pieces(0)
    start(z_copy(1))
    spread(0)
    loads[2].wait()
    for h in range(HEADS):
        s = jnp.where(causal, dot(head(q_ref, h), head(k_ref, h), NT), 0.0).astype(BF16)
        scores[h] = s
        local_part[h] = dot(s, head(v_ref, h), NN)
    send_totals(0)
    for d in range(2, planes):
        start(z_copy(d))
    loads[4].wait()
    for i in range(planes):
        cot_t[i] = cot_ref[:, i * width:(i + 1) * width].T.reshape(4, 2, rows, tokens)
    start(exchanges[0])
    spread(1)
    send_prefixes(0)
    for i in range(planes):
        cot_sel[i, :tokens] = cot_t[i, :, core].reshape(4 * rows, tokens).T
    pass_on(0)
    spread(2)
    loads[3].wait()
    wait_state(0)
    for h in range(HEADS):
        a = (local_part[h] + dot(head(q_ref, h), state_of(0, h), NN)) * scale
        att[:, h * HEAD:(h + 1) * HEAD] = a.astype(BF16)
    start(exchanges[1])
    pass_on(1)
    for d in range(3, planes):
        spread(d)
    att_pair[:tokens] = att[...]
    exchanges[0].wait_recv()
    for i in range(planes):
        cot_sel[i, tokens:] = cot_sib[i].reshape(4 * rows, tokens).T
    for d in range(2, planes):
        pass_on(d)
    exchanges[1].wait_recv()
    att_pair[tokens:] = att_sib[...]

    half = planes // 2
    for d in range(half):
        reduce_2(targets[d])
    grad_acc = jnp.zeros((2 * tokens, HEADS * HEAD), F32)
    for d in range(planes):
        pass_diag(d)
        w = full_w[plane_before(d), :, core].reshape(4 * rows, HEADS * HEAD)
        grad_acc = grad_acc + dot(cot_sel[plane_before(d)], w, NN)
    grad_sib[...] = grad_acc[tokens:]
    start(exchanges[2])
    own_grad = grad_acc[:tokens]
    exchanges[2].wait_recv()
    grad[...] = ((own_grad + grad_in[...]) * scale).astype(BF16)
    pieces(1, q_ref, grad)
    send_pieces(1)

    stores = []

    def put(i, src, dst):
        c = pltpu.make_async_copy(src, dst, store.at[i])
        c.start()
        stores.append(c)

    def mix(i):
        w = full_w[i].reshape(width, w_ref.shape[1])
        cols = pl.ds(i * width, width)
        mixed_ref[:, cols] = dot(att[...], w, NT).astype(BF16)
        put(4 + i, mixed_ref.at[:, cols], mixed_hbm.at[:, cols])

    for d in range(half):
        reduce_3(targets[d])
    for d in range(half, planes):
        reduce_2(targets[d])
    send_totals(1)
    for h in range(HEADS):
        cols = slice(h * HEAD, (h + 1) * HEAD)
        q, k, v, g = head(q_ref, h), head(k_ref, h), head(v_ref, h), head(grad, h)
        gs = jnp.where(causal, dot(g, v, NT), 0.0).astype(BF16)
        dq_ref[:, cols] = (dot(gs, k, NN) + dot(g, state_of(0, h), NT)).astype(BF16)
        dk_part[:, cols] = dot(gs, q, TN)
        dv_part[:, cols] = dot(scores[h], g, TN)
    send_prefixes(1)
    put(0, dq_ref, dq_hbm)
    for d in range(half):
        reduce_4(targets[d])
    for d in range(half, planes):
        reduce_3(targets[d])
    for d in range(planes):
        for i in range(4):
            sib_copy(d, i).wait_recv()
    for i in range(half):
        mix(i)
    for d in range(half, planes - 1):
        reduce_4(targets[d])
    wait_state(1)
    for h in range(HEADS):
        cols = slice(h * HEAD, (h + 1) * HEAD)
        k, v = head(k_ref, h), head(v_ref, h)
        dk_ref[:, cols] = (dk_part[:, cols] + dot(v, state_of(1, h), NT)).astype(BF16)
        dv_ref[:, cols] = (dv_part[:, cols] + dot(k, state_of(1, h), NN)).astype(BF16)
    put(1, dk_ref, dk_hbm)
    put(2, dv_ref, dv_hbm)
    for i in range(half, planes):
        mix(i)
    reduce_4(0)
    reduce_5()
    put(3, wg_ref, wg_hbm)
    for c in sent:
        c.wait_send()
    for c in stores:
        c.wait()


def place(*refs):
    load, store = refs[15:]
    loads = [pltpu.make_async_copy(refs[i], refs[10 + i], load.at[i]) for i in range(5)]
    stores = [pltpu.make_async_copy(refs[10 + i], refs[5 + i], store.at[i]) for i in range(5)]
    for c in loads:
        c.start()
    for i in range(5):
        loads[i].wait()
        stores[i].start()
    for c in stores:
        c.wait()


def body(planes, queries, keys, values, out_weight, cotangent):
    tokens, hf = queries.shape
    rows = out_weight.shape[0]
    half = HEAD // 2
    dma = pltpu.SemaphoreType.DMA
    hbm = pl.BlockSpec(memory_space=pl.ANY)
    blocks = pltpu.VMEM((planes, rows, hf), BF16)
    results = pl.pallas_call(
        functools.partial(kernel, planes),
        out_shape=(
            jax.ShapeDtypeStruct(cotangent.shape, BF16),
            jax.ShapeDtypeStruct(queries.shape, BF16),
            jax.ShapeDtypeStruct(queries.shape, BF16),
            jax.ShapeDtypeStruct(queries.shape, BF16),
            jax.ShapeDtypeStruct(out_weight.shape, F32),
        ),
        in_specs=[hbm] * 5,
        out_specs=(hbm,) * 5,
        scratch_shapes=[
            pltpu.VMEM(cotangent.shape, BF16),
            pltpu.VMEM(queries.shape, BF16),
            pltpu.VMEM(queries.shape, BF16),
            pltpu.VMEM(queries.shape, BF16),
            pltpu.VMEM(out_weight.shape, F32),
            dma((4 + planes,)),
            pltpu.VMEM(queries.shape, BF16),
            pltpu.VMEM(queries.shape, BF16),
            pltpu.VMEM(queries.shape, BF16),
            pltpu.VMEM(cotangent.shape, BF16),
            pltpu.VMEM((planes, 4, 2, rows, tokens), BF16),
            dma((5,)),
            pltpu.VMEM((planes, 4, rows, tokens), BF16),
            pltpu.VMEM((planes, 2 * tokens, 4 * rows), BF16),
            pltpu.VMEM((2 * tokens, hf), BF16),
            pltpu.VMEM((tokens, hf), BF16),
            pltpu.VMEM((tokens, hf), F32),
            pltpu.VMEM((tokens, hf), F32),
            pltpu.VMEM((tokens, hf), F32),
            pltpu.VMEM((tokens, hf), F32),
            pltpu.VMEM((planes, 4, 2, rows, hf), BF16),
            pltpu.VMEM((planes, 4, rows, hf), BF16),
            blocks, blocks, blocks, blocks, blocks,
            pltpu.VMEM((rows, hf), F32),
            pltpu.VMEM((HEADS, tokens, tokens), BF16),
            pltpu.VMEM((HEADS, tokens, HEAD), F32),
            pltpu.VMEM((tokens, hf), BF16),
            pltpu.VMEM((tokens, hf), BF16),
            pltpu.VMEM((2, GROUP, half, HEAD), BF16),
            pltpu.VMEM((2, GROUP, half, HEAD), BF16),
            pltpu.VMEM((2, half, HEAD), F32),
            pltpu.VMEM((2, planes, half, HEAD), F32),
            pltpu.VMEM((2, GROUP, half, HEAD), BF16),
            pltpu.VMEM((2, GROUP, half, HEAD), BF16),
            dma((2, GROUP)), dma((2, GROUP)),
            dma((2, planes)), dma((2, planes)),
            dma((2, GROUP)), dma((2, GROUP)),
        ] + [dma((planes,))] * 8 + [dma((planes, 4))] * 2 + [dma((3,))] * 2 + [dma((planes,))] * 8,
        compiler_params=pltpu.CompilerParams(
            collective_id=0, has_side_effects=True, vmem_limit_bytes=60 * 1024 * 1024
        ),
    )(queries, keys, values, out_weight, cotangent)
    return pl.pallas_call(
        place,
        out_shape=[jax.ShapeDtypeStruct(r.shape, r.dtype) for r in results],
        in_specs=[hbm] * 5,
        out_specs=[hbm] * 5,
        scratch_shapes=[pltpu.VMEM(r.shape, r.dtype) for r in results] + [dma((5,))] * 2,
        compiler_params=pltpu.CompilerParams(vmem_limit_bytes=60 * 1024 * 1024),
    )(*results)


def solution(mesh):
    planes = mesh.shape["ctx"] // GROUP
    spec = P("ctx", None)
    return jax.shard_map(
        functools.partial(body, planes),
        mesh=mesh,
        in_specs=(spec,) * 5,
        out_specs=(spec,) * 5,
        check_vma=False,
    )
```

```python
import functools

import jax
import jax.numpy as jnp
from jax import lax
from jax.experimental import pallas as pl
from jax.experimental.pallas import tpu as pltpu
from jax.sharding import PartitionSpec as P

HEADS = 4
HEAD = 128
GROUP = 8
F32 = jnp.float32
BF16 = jnp.bfloat16
MESH = pl.DeviceIdType.MESH


def dot(x, y, dims):
    return lax.dot_general(x, y, (dims, ((), ())), preferred_element_type=F32)


NN = ((1,), (0,))
NT = ((1,), (1,))
TN = ((0,), (0,))


def kernel(
    planes,
    q_hbm, k_hbm, v_hbm, w_ref, cot_hbm,
    mixed_hbm, dq_hbm, dk_hbm, dv_hbm, wg_hbm,
    mixed_ref, dq_ref, dk_ref, dv_ref, wg_ref, store,
    q_ref, k_ref, v_ref, cot_ref, cot_t, load,
    cot_sib, cot_sel, att_pair, att_sib, grad_sib, grad_in, dk_part, dv_part,
    full_w, summed, from_diag, from_x, from_y, to_plane, from_plane, own_sum,
    scores, local_part, att, grad,
    piece_out, piece_in, total_out, totals, prefix_out, state,
    p1_send, p1_recv, p2_send, p2_recv, p3_send, p3_recv,
    z_send, z_recv, x_send, x_recv, y_send, y_recv, g_send, g_recv, s_send, s_recv,
    e_send, e_recv, rd_send, rd_recv, rx_send, rx_recv, ry_send, ry_recv, rz_send, rz_recv,
):
    tokens = q_ref.shape[0]
    rows = w_ref.shape[0]
    width = GROUP * rows
    me = lax.axis_index("ctx")
    plane = lax.div(me, GROUP)
    member = lax.rem(me, GROUP)
    core = lax.rem(member, 2)
    quad = lax.div(member, 2)
    quad_x = lax.rem(quad, 2)
    quad_y = lax.div(quad, 2)
    to_x = 1 - 2 * quad_x
    to_y = 2 - 4 * quad_y
    col_x = quad + to_x
    col_y = quad + to_y
    col_d = 3 - quad
    x_dev = me + 2 * to_x
    y_dev = me + 2 * to_y
    sib = me + 1 - 2 * core
    other = 1 - core

    def mate(r):
        return lax.rem(member + r, GROUP)

    def mate_dev(r):
        return plane * GROUP + mate(r)

    def plane_at(d):
        return lax.rem(plane + d, planes)

    def plane_before(d):
        return lax.rem(plane + planes - d, planes)

    def plane_dev(d):
        return plane_at(d) * GROUP + member

    def copy(src, dst, send, recv, device):
        return pltpu.make_async_remote_copy(
            src_ref=src, dst_ref=dst, send_sem=send, recv_sem=recv,
            device_id=(device,), device_id_type=MESH,
        )

    sent = []

    def start(c):
        c.start()
        sent.append(c)

    loads = [
        pltpu.make_async_copy(src, dst, load.at[i])
        for i, (src, dst) in enumerate((
            (k_hbm, k_ref), (v_hbm, v_ref), (q_hbm, q_ref),
            (w_ref, full_w.at[plane, quad, core]), (cot_hbm, cot_ref),
        ))
    ]
    for c in loads:
        c.start()

    barrier = pltpu.get_barrier_semaphore()
    for r in range(1, GROUP):
        pl.semaphore_signal(barrier, inc=1, device_id=(mate_dev(r),), device_id_type=MESH)
    for d in range(1, planes):
        pl.semaphore_signal(barrier, inc=1, device_id=(plane_dev(d),), device_id_type=MESH)

    def head(ref, h):
        return ref[:, h * HEAD:(h + 1) * HEAD]

    def pieces(way, left, right):
        for h in range(HEADS):
            outer = dot(head(left, h), head(right, h), TN).astype(BF16)
            piece_out[way, 2 * h:2 * h + 2] = outer.reshape(2, HEAD // 2, HEAD)

    def piece_copy(way, r):
        return copy(piece_out.at[way, mate(r)], piece_in.at[way, member],
                    p1_send.at[way, r], p1_recv.at[way, r], mate_dev(r))

    def send_pieces(way):
        for r in range(1, GROUP):
            start(piece_copy(way, r))
        piece_in[way, member] = piece_out[way, member]

    def total_copy(way, d):
        return copy(total_out.at[way], totals.at[way, plane],
                    p2_send.at[way, d], p2_recv.at[way, d], plane_dev(d))

    def send_totals(way):
        for r in range(1, GROUP):
            piece_copy(way, r).wait_recv()
        total = piece_in[way, 0].astype(F32)
        for j in range(1, GROUP):
            total = total + piece_in[way, j].astype(F32)
        total_out[way] = total
        totals[way, plane] = total
        for d in range(1, planes):
            start(total_copy(way, d))

    def prefix_copy(way, r):
        return copy(prefix_out.at[way, mate(r)], state.at[way, member],
                    p3_send.at[way, r], p3_recv.at[way, r], mate_dev(r))

    def send_prefixes(way):
        for d in range(1, planes):
            total_copy(way, d).wait_recv()
        run = jnp.zeros((HEAD // 2, HEAD), F32)
        for i in range(planes):
            counts = (i < plane) if way == 0 else (i > plane)
            run = run + jnp.where(counts, totals[way, i], 0.0)
        for j in (range(GROUP) if way == 0 else range(GROUP - 1, -1, -1)):
            prefix_out[way, j] = run.astype(BF16)
            run = run + piece_in[way, j].astype(F32)
        for r in range(1, GROUP):
            start(prefix_copy(way, r))
        state[way, member] = prefix_out[way, member]

    def wait_state(way):
        for r in range(1, GROUP):
            prefix_copy(way, r).wait_recv()

    def state_of(way, h):
        return state[way, 2 * h:2 * h + 2].reshape(HEAD, HEAD)

    def z_copy(d):
        return copy(w_ref, full_w.at[plane, quad, core], z_send.at[d], z_recv.at[d], plane_dev(d))

    def block(d, col):
        return full_w.at[plane_before(d), col, core]

    def move(d, col, sems, device, first=False):
        send, recv = sems
        return copy(w_ref if first else block(d, col), block(d, col), send, recv, device)

    def x_copy(d, first=False):
        return move(d, quad, (x_send.at[d], x_recv.at[d]), x_dev, first)

    def y_copy(d, first=False):
        return move(d, quad, (y_send.at[d], y_recv.at[d]), y_dev, first)

    def diag_copy(d):
        if d % 2 == 0:
            return move(d, col_y, (g_send.at[d], g_recv.at[d]), x_dev)
        return move(d, col_x, (g_send.at[d], g_recv.at[d]), y_dev)

    def sib_copy(d, i, first=False):
        col = (quad, col_x, col_y, col_d)[i]
        return move(d, col, (s_send.at[d, i], s_recv.at[d, i]), sib, first)

    def spread(d):
        if d:
            z_copy(d).wait_recv()
        start(x_copy(d, d == 0))
        start(y_copy(d, d == 0))
        start(sib_copy(d, 0, d == 0))

    def pass_on(d):
        x_copy(d).wait_recv()
        if d % 2:
            start(diag_copy(d))
        start(sib_copy(d, 1))
        y_copy(d).wait_recv()
        if d % 2 == 0:
            start(diag_copy(d))
        start(sib_copy(d, 2))

    def pass_diag(d):
        diag_copy(d).wait_recv()
        start(sib_copy(d, 3))

    exchanges = [
        copy(src, dst, e_send.at[i], e_recv.at[i], sib)
        for i, (src, dst) in enumerate((
            (cot_t.at[:, :, other], cot_sib), (att, att_sib), (grad_sib, grad_in),
        ))
    ]

    def rd_copy(d):
        return copy(summed.at[d, col_d], from_diag.at[d], rd_send.at[d], rd_recv.at[d],
                    y_dev if d % 2 else x_dev)

    def rx_copy(d):
        return copy(summed.at[d, col_x], from_x.at[d], rx_send.at[d], rx_recv.at[d], x_dev)

    def ry_copy(d):
        return copy(summed.at[d, col_y], from_y.at[d], ry_send.at[d], ry_recv.at[d], y_dev)

    def reduce_2(d):
        a = plane_at(d)
        tall = jnp.concatenate([cot_t[a, :, core], cot_sib[a]], axis=-1)
        term = dot(tall.reshape(4 * rows, 2 * tokens), att_pair[...], NN).astype(BF16)
        summed[d] = term.reshape(4, rows, HEADS * HEAD)
        start(rd_copy(d))
        start(ry_copy(d) if d % 2 else rx_copy(d))

    def reduce_3(d):
        rd_copy(d).wait_recv()
        col = col_x if d % 2 else col_y
        both = summed[d, col].astype(F32) + from_diag[d].astype(F32)
        summed[d, col] = both.astype(BF16)
        start(rx_copy(d) if d % 2 else ry_copy(d))

    def rz_copy(d):
        return copy(to_plane.at[d], from_plane.at[d], rz_send.at[d], rz_recv.at[d], plane_dev(d))

    def reduce_4(d):
        rx_copy(d).wait_recv()
        ry_copy(d).wait_recv()
        total = summed[d, quad].astype(F32) + from_x[d].astype(F32) + from_y[d].astype(F32)
        if d:
            to_plane[d] = total.astype(BF16)
            start(rz_copy(d))
        else:
            own_sum[...] = total

    def reduce_5():
        total = own_sum[...]
        for d in range(1, planes):
            rz_copy(d).wait_recv()
            total = total + from_plane[d].astype(F32)
        wg_ref[...] = total

    targets = list(range(2, planes)) + [1, 0]
    sources = [0, 1] + list(range(planes - 1, 1, -1))

    position = me * tokens + lax.broadcasted_iota(jnp.int32, (tokens, 1), 0)
    scale = lax.rsqrt(HEAD * (position + 1).astype(F32))
    causal = lax.broadcasted_iota(jnp.int32, (tokens, tokens), 0) >= lax.broadcasted_iota(
        jnp.int32, (tokens, tokens), 1
    )

    loads[0].wait()
    loads[1].wait()
    pieces(0, k_ref, v_ref)
    pl.semaphore_wait(barrier, GROUP - 1 + planes - 1)
    send_pieces(0)
    start(z_copy(1))
    spread(0)
    loads[2].wait()
    for h in range(HEADS):
        s = jnp.where(causal, dot(head(q_ref, h), head(k_ref, h), NT), 0.0).astype(BF16)
        scores[h] = s
        local_part[h] = dot(s, head(v_ref, h), NN)
    send_totals(0)
    for d in sources[2:]:
        start(z_copy(d))
    loads[4].wait()
    for i in range(planes):
        cot_t[i] = cot_ref[:, i * width:(i + 1) * width].T.reshape(4, 2, rows, tokens)
    start(exchanges[0])
    spread(1)
    send_prefixes(0)
    for i in range(planes):
        cot_sel[i, :tokens] = cot_t[i, :, core].reshape(4 * rows, tokens).T
    pass_on(0)
    spread(sources[2])
    loads[3].wait()
    wait_state(0)
    for h in range(HEADS):
        a = (local_part[h] + dot(head(q_ref, h), state_of(0, h), NN)) * scale
        att[:, h * HEAD:(h + 1) * HEAD] = a.astype(BF16)
    start(exchanges[1])
    pass_on(1)
    for d in sources[3:]:
        spread(d)
    att_pair[:tokens] = att[...]
    exchanges[0].wait_recv()
    for i in range(planes):
        cot_sel[i, tokens:] = cot_sib[i].reshape(4 * rows, tokens).T
    for d in sources[2:]:
        pass_on(d)
    exchanges[1].wait_recv()
    att_pair[tokens:] = att_sib[...]

    half = planes // 2
    for d in range(half):
        reduce_2(targets[d])
    grad_acc = jnp.zeros((2 * tokens, HEADS * HEAD), F32)
    for d in sources:
        pass_diag(d)
        w = full_w[plane_before(d), :, core].reshape(4 * rows, HEADS * HEAD)
        grad_acc = grad_acc + dot(cot_sel[plane_before(d)], w, NN)
    grad_sib[...] = grad_acc[tokens:]
    start(exchanges[2])
    own_grad = grad_acc[:tokens]
    exchanges[2].wait_recv()
    grad[...] = ((own_grad + grad_in[...]) * scale).astype(BF16)
    pieces(1, q_ref, grad)
    send_pieces(1)

    stores = []

    def put(i, src, dst):
        c = pltpu.make_async_copy(src, dst, store.at[i])
        c.start()
        stores.append(c)

    def mix(i):
        w = full_w[i].reshape(width, w_ref.shape[1])
        cols = pl.ds(i * width, width)
        mixed_ref[:, cols] = dot(att[...], w, NT).astype(BF16)
        put(4 + i, mixed_ref.at[:, cols], mixed_hbm.at[:, cols])

    for d in range(half):
        reduce_3(targets[d])
    for d in range(half, planes):
        reduce_2(targets[d])
    send_totals(1)
    for h in range(HEADS):
        cols = slice(h * HEAD, (h + 1) * HEAD)
        q, k, v, g = head(q_ref, h), head(k_ref, h), head(v_ref, h), head(grad, h)
        gs = jnp.where(causal, dot(g, v, NT), 0.0).astype(BF16)
        dq_ref[:, cols] = (dot(gs, k, NN) + dot(g, state_of(0, h), NT)).astype(BF16)
        dk_part[:, cols] = dot(gs, q, TN)
        dv_part[:, cols] = dot(scores[h], g, TN)
    send_prefixes(1)
    put(0, dq_ref, dq_hbm)
    for d in range(half):
        reduce_4(targets[d])
    for d in range(half, planes):
        reduce_3(targets[d])
    for d in range(planes):
        for i in range(4):
            sib_copy(d, i).wait_recv()
    mix(0)
    for d in range(half, planes - 1):
        reduce_4(targets[d])
    wait_state(1)
    for h in range(HEADS):
        cols = slice(h * HEAD, (h + 1) * HEAD)
        k, v = head(k_ref, h), head(v_ref, h)
        dk_ref[:, cols] = (dk_part[:, cols] + dot(v, state_of(1, h), NT)).astype(BF16)
        dv_ref[:, cols] = (dv_part[:, cols] + dot(k, state_of(1, h), NN)).astype(BF16)
    put(1, dk_ref, dk_hbm)
    put(2, dv_ref, dv_hbm)
    for i in range(1, planes):
        mix(i)
    reduce_4(0)
    reduce_5()
    put(3, wg_ref, wg_hbm)
    for c in sent:
        c.wait_send()
    for c in stores:
        c.wait()


def place(*refs):
    load, store = refs[15:]
    loads = [pltpu.make_async_copy(refs[i], refs[10 + i], load.at[i]) for i in range(5)]
    stores = [pltpu.make_async_copy(refs[10 + i], refs[5 + i], store.at[i]) for i in range(5)]
    for c in loads:
        c.start()
    for i in range(5):
        loads[i].wait()
        stores[i].start()
    for c in stores:
        c.wait()


def body(planes, queries, keys, values, out_weight, cotangent):
    tokens, hf = queries.shape
    rows = out_weight.shape[0]
    half = HEAD // 2
    dma = pltpu.SemaphoreType.DMA
    hbm = pl.BlockSpec(memory_space=pl.ANY)
    blocks = pltpu.VMEM((planes, rows, hf), BF16)
    results = pl.pallas_call(
        functools.partial(kernel, planes),
        out_shape=(
            jax.ShapeDtypeStruct(cotangent.shape, BF16),
            jax.ShapeDtypeStruct(queries.shape, BF16),
            jax.ShapeDtypeStruct(queries.shape, BF16),
            jax.ShapeDtypeStruct(queries.shape, BF16),
            jax.ShapeDtypeStruct(out_weight.shape, F32),
        ),
        in_specs=[hbm] * 5,
        out_specs=(hbm,) * 5,
        scratch_shapes=[
            pltpu.VMEM(cotangent.shape, BF16),
            pltpu.VMEM(queries.shape, BF16),
            pltpu.VMEM(queries.shape, BF16),
            pltpu.VMEM(queries.shape, BF16),
            pltpu.VMEM(out_weight.shape, F32),
            dma((4 + planes,)),
            pltpu.VMEM(queries.shape, BF16),
            pltpu.VMEM(queries.shape, BF16),
            pltpu.VMEM(queries.shape, BF16),
            pltpu.VMEM(cotangent.shape, BF16),
            pltpu.VMEM((planes, 4, 2, rows, tokens), BF16),
            dma((5,)),
            pltpu.VMEM((planes, 4, rows, tokens), BF16),
            pltpu.VMEM((planes, 2 * tokens, 4 * rows), BF16),
            pltpu.VMEM((2 * tokens, hf), BF16),
            pltpu.VMEM((tokens, hf), BF16),
            pltpu.VMEM((tokens, hf), F32),
            pltpu.VMEM((tokens, hf), F32),
            pltpu.VMEM((tokens, hf), F32),
            pltpu.VMEM((tokens, hf), F32),
            pltpu.VMEM((planes, 4, 2, rows, hf), BF16),
            pltpu.VMEM((planes, 4, rows, hf), BF16),
            blocks, blocks, blocks, blocks, blocks,
            pltpu.VMEM((rows, hf), F32),
            pltpu.VMEM((HEADS, tokens, tokens), BF16),
            pltpu.VMEM((HEADS, tokens, HEAD), F32),
            pltpu.VMEM((tokens, hf), BF16),
            pltpu.VMEM((tokens, hf), BF16),
            pltpu.VMEM((2, GROUP, half, HEAD), BF16),
            pltpu.VMEM((2, GROUP, half, HEAD), BF16),
            pltpu.VMEM((2, half, HEAD), F32),
            pltpu.VMEM((2, planes, half, HEAD), F32),
            pltpu.VMEM((2, GROUP, half, HEAD), BF16),
            pltpu.VMEM((2, GROUP, half, HEAD), BF16),
            dma((2, GROUP)), dma((2, GROUP)),
            dma((2, planes)), dma((2, planes)),
            dma((2, GROUP)), dma((2, GROUP)),
        ] + [dma((planes,))] * 8 + [dma((planes, 4))] * 2 + [dma((3,))] * 2 + [dma((planes,))] * 8,
        compiler_params=pltpu.CompilerParams(
            collective_id=0, has_side_effects=True, vmem_limit_bytes=60 * 1024 * 1024
        ),
    )(queries, keys, values, out_weight, cotangent)
    return pl.pallas_call(
        place,
        out_shape=[jax.ShapeDtypeStruct(r.shape, r.dtype) for r in results],
        in_specs=[hbm] * 5,
        out_specs=[hbm] * 5,
        scratch_shapes=[pltpu.VMEM(r.shape, r.dtype) for r in results] + [dma((5,))] * 2,
        compiler_params=pltpu.CompilerParams(vmem_limit_bytes=60 * 1024 * 1024),
    )(*results)


def solution(mesh):
    planes = mesh.shape["ctx"] // GROUP
    spec = P("ctx", None)
    return jax.shard_map(
        functools.partial(body, planes),
        mesh=mesh,
        in_specs=(spec,) * 5,
        out_specs=(spec,) * 5,
        check_vma=False,
    )
```

```python
import functools

import jax
import jax.numpy as jnp
from jax import lax
from jax.experimental import pallas as pl
from jax.experimental.pallas import tpu as pltpu
from jax.sharding import PartitionSpec as P

HEADS = 4
HEAD = 128
GROUP = 8
F32 = jnp.float32
BF16 = jnp.bfloat16
MESH = pl.DeviceIdType.MESH


def dot(x, y, dims):
    return lax.dot_general(x, y, (dims, ((), ())), preferred_element_type=F32)


NN = ((1,), (0,))
NT = ((1,), (1,))
TN = ((0,), (0,))


def kernel(
    planes,
    q_hbm, k_hbm, v_hbm, w_ref, cot_hbm,
    mixed_hbm, dq_hbm, dk_hbm, dv_hbm, wg_hbm,
    mixed_ref, dq_ref, dk_ref, dv_ref, wg_ref, store,
    q_ref, k_ref, v_ref, cot_ref, cot_t, load,
    cot_sib, cot_sel, att_pair, att_sib, grad_sib, grad_in, dk_part, dv_part,
    full_w, summed, from_diag, from_x, from_y, to_plane, from_plane, own_sum,
    scores, local_part, att, grad,
    piece_out, piece_in, total_out, totals, prefix_out, state,
    p1_send, p1_recv, p2_send, p2_recv, p3_send, p3_recv,
    z_send, z_recv, x_send, x_recv, y_send, y_recv, g_send, g_recv, s_send, s_recv,
    e_send, e_recv, rd_send, rd_recv, rx_send, rx_recv, ry_send, ry_recv, rz_send, rz_recv,
):
    tokens = q_ref.shape[0]
    rows = w_ref.shape[0]
    width = GROUP * rows
    me = lax.axis_index("ctx")
    plane = lax.div(me, GROUP)
    member = lax.rem(me, GROUP)
    core = lax.rem(member, 2)
    quad = lax.div(member, 2)
    quad_x = lax.rem(quad, 2)
    quad_y = lax.div(quad, 2)
    to_x = 1 - 2 * quad_x
    to_y = 2 - 4 * quad_y
    col_x = quad + to_x
    col_y = quad + to_y
    col_d = 3 - quad
    x_dev = me + 2 * to_x
    y_dev = me + 2 * to_y
    sib = me + 1 - 2 * core
    other = 1 - core

    def mate(r):
        return lax.rem(member + r, GROUP)

    def mate_dev(r):
        return plane * GROUP + mate(r)

    def plane_at(d):
        return lax.rem(plane + d, planes)

    def plane_before(d):
        return lax.rem(plane + planes - d, planes)

    def plane_dev(d):
        return plane_at(d) * GROUP + member

    def copy(src, dst, send, recv, device):
        return pltpu.make_async_remote_copy(
            src_ref=src, dst_ref=dst, send_sem=send, recv_sem=recv,
            device_id=(device,), device_id_type=MESH,
        )

    sent = []

    def start(c):
        c.start()
        sent.append(c)

    loads = [
        pltpu.make_async_copy(src, dst, load.at[i])
        for i, (src, dst) in enumerate((
            (k_hbm, k_ref), (v_hbm, v_ref), (q_hbm, q_ref),
            (w_ref, full_w.at[plane, quad, core]), (cot_hbm, cot_ref),
        ))
    ]
    for c in loads:
        c.start()

    barrier = pltpu.get_barrier_semaphore()
    for r in range(1, GROUP):
        pl.semaphore_signal(barrier, inc=1, device_id=(mate_dev(r),), device_id_type=MESH)
    for d in range(1, planes):
        pl.semaphore_signal(barrier, inc=1, device_id=(plane_dev(d),), device_id_type=MESH)

    def head(ref, h):
        return ref[:, h * HEAD:(h + 1) * HEAD]

    def pieces(way, left, right):
        for h in range(HEADS):
            outer = dot(head(left, h), head(right, h), TN).astype(BF16)
            piece_out[way, 2 * h:2 * h + 2] = outer.reshape(2, HEAD // 2, HEAD)

    def piece_copy(way, r):
        return copy(piece_out.at[way, mate(r)], piece_in.at[way, member],
                    p1_send.at[way, r], p1_recv.at[way, r], mate_dev(r))

    def send_pieces(way):
        for r in range(1, GROUP):
            start(piece_copy(way, r))
        piece_in[way, member] = piece_out[way, member]

    def total_copy(way, d):
        return copy(total_out.at[way], totals.at[way, plane],
                    p2_send.at[way, d], p2_recv.at[way, d], plane_dev(d))

    def send_totals(way):
        for r in range(1, GROUP):
            piece_copy(way, r).wait_recv()
        total = piece_in[way, 0].astype(F32)
        for j in range(1, GROUP):
            total = total + piece_in[way, j].astype(F32)
        total_out[way] = total
        totals[way, plane] = total
        for d in range(1, planes):
            start(total_copy(way, d))

    def prefix_copy(way, r):
        return copy(prefix_out.at[way, mate(r)], state.at[way, member],
                    p3_send.at[way, r], p3_recv.at[way, r], mate_dev(r))

    def send_prefixes(way):
        for d in range(1, planes):
            total_copy(way, d).wait_recv()
        run = jnp.zeros((HEAD // 2, HEAD), F32)
        for i in range(planes):
            counts = (i < plane) if way == 0 else (i > plane)
            run = run + jnp.where(counts, totals[way, i], 0.0)
        for j in (range(GROUP) if way == 0 else range(GROUP - 1, -1, -1)):
            prefix_out[way, j] = run.astype(BF16)
            run = run + piece_in[way, j].astype(F32)
        for r in range(1, GROUP):
            start(prefix_copy(way, r))
        state[way, member] = prefix_out[way, member]

    def wait_state(way):
        for r in range(1, GROUP):
            prefix_copy(way, r).wait_recv()

    def state_of(way, h):
        return state[way, 2 * h:2 * h + 2].reshape(HEAD, HEAD)

    def z_copy(d):
        return copy(w_ref, full_w.at[plane, quad, core], z_send.at[d], z_recv.at[d], plane_dev(d))

    def block(d, col):
        return full_w.at[plane_before(d), col, core]

    def move(d, col, sems, device, first=False):
        send, recv = sems
        return copy(w_ref if first else block(d, col), block(d, col), send, recv, device)

    def x_copy(d, first=False):
        return move(d, quad, (x_send.at[d], x_recv.at[d]), x_dev, first)

    def y_copy(d, first=False):
        return move(d, quad, (y_send.at[d], y_recv.at[d]), y_dev, first)

    def diag_copy(d):
        if d % 2 == 0:
            return move(d, col_y, (g_send.at[d], g_recv.at[d]), x_dev)
        return move(d, col_x, (g_send.at[d], g_recv.at[d]), y_dev)

    def sib_copy(d, i, first=False):
        col = (quad, col_x, col_y, col_d)[i]
        return move(d, col, (s_send.at[d, i], s_recv.at[d, i]), sib, first)

    def spread(d):
        if d:
            z_copy(d).wait_recv()
        start(x_copy(d, d == 0))
        start(y_copy(d, d == 0))
        start(sib_copy(d, 0, d == 0))

    def pass_on(d):
        x_copy(d).wait_recv()
        if d % 2:
            start(diag_copy(d))
        start(sib_copy(d, 1))
        y_copy(d).wait_recv()
        if d % 2 == 0:
            start(diag_copy(d))
        start(sib_copy(d, 2))

    def pass_diag(d):
        diag_copy(d).wait_recv()
        start(sib_copy(d, 3))

    exchanges = [
        copy(src, dst, e_send.at[i], e_recv.at[i], sib)
        for i, (src, dst) in enumerate((
            (cot_t.at[:, :, other], cot_sib), (att, att_sib), (grad_sib, grad_in),
        ))
    ]

    def rd_copy(d):
        return copy(summed.at[d, col_d], from_diag.at[d], rd_send.at[d], rd_recv.at[d],
                    y_dev if d % 2 else x_dev)

    def rx_copy(d):
        return copy(summed.at[d, col_x], from_x.at[d], rx_send.at[d], rx_recv.at[d], x_dev)

    def ry_copy(d):
        return copy(summed.at[d, col_y], from_y.at[d], ry_send.at[d], ry_recv.at[d], y_dev)

    def reduce_2(d):
        a = plane_at(d)
        tall = jnp.concatenate([cot_t[a, :, core], cot_sib[a]], axis=-1)
        term = dot(tall.reshape(4 * rows, 2 * tokens), att_pair[...], NN).astype(BF16)
        summed[d] = term.reshape(4, rows, HEADS * HEAD)
        start(rd_copy(d))
        start(ry_copy(d) if d % 2 else rx_copy(d))

    def reduce_3(d):
        rd_copy(d).wait_recv()
        col = col_x if d % 2 else col_y
        both = summed[d, col].astype(F32) + from_diag[d].astype(F32)
        summed[d, col] = both.astype(BF16)
        start(rx_copy(d) if d % 2 else ry_copy(d))

    def rz_copy(d):
        return copy(to_plane.at[d], from_plane.at[d], rz_send.at[d], rz_recv.at[d], plane_dev(d))

    def reduce_4(d):
        rx_copy(d).wait_recv()
        ry_copy(d).wait_recv()
        total = summed[d, quad].astype(F32) + from_x[d].astype(F32) + from_y[d].astype(F32)
        if d:
            to_plane[d] = total.astype(BF16)
            start(rz_copy(d))
        else:
            own_sum[...] = total

    def reduce_5():
        total = own_sum[...]
        for d in range(1, planes):
            rz_copy(d).wait_recv()
            total = total + from_plane[d].astype(F32)
        wg_ref[...] = total

    targets = list(range(2, planes)) + [1, 0]
    sources = [0, 1] + list(range(planes - 1, 1, -1))

    position = me * tokens + lax.broadcasted_iota(jnp.int32, (tokens, 1), 0)
    scale = lax.rsqrt(HEAD * (position + 1).astype(F32))
    causal = lax.broadcasted_iota(jnp.int32, (tokens, tokens), 0) >= lax.broadcasted_iota(
        jnp.int32, (tokens, tokens), 1
    )

    loads[0].wait()
    loads[1].wait()
    pieces(0, k_ref, v_ref)
    pl.semaphore_wait(barrier, GROUP - 1 + planes - 1)
    send_pieces(0)
    start(z_copy(1))
    spread(0)
    loads[2].wait()
    for h in range(HEADS):
        s = jnp.where(causal, dot(head(q_ref, h), head(k_ref, h), NT), 0.0).astype(BF16)
        scores[h] = s
        local_part[h] = dot(s, head(v_ref, h), NN)
    send_totals(0)
    for d in sources[2:]:
        start(z_copy(d))
    loads[4].wait()
    for i in range(planes):
        cot_t[i] = cot_ref[:, i * width:(i + 1) * width].T.reshape(4, 2, rows, tokens)
    start(exchanges[0])
    spread(1)
    send_prefixes(0)
    for i in range(planes):
        cot_sel[i, :tokens] = cot_t[i, :, core].reshape(4 * rows, tokens).T
    pass_on(0)
    spread(sources[2])
    loads[3].wait()
    wait_state(0)
    for h in range(HEADS):
        a = (local_part[h] + dot(head(q_ref, h), state_of(0, h), NN)) * scale
        att[:, h * HEAD:(h + 1) * HEAD] = a.astype(BF16)
    start(exchanges[1])
    pass_on(1)
    for d in sources[3:]:
        spread(d)
    att_pair[:tokens] = att[...]
    exchanges[0].wait_recv()
    for i in range(planes):
        cot_sel[i, tokens:] = cot_sib[i].reshape(4 * rows, tokens).T
    for d in sources[2:]:
        pass_on(d)
    exchanges[1].wait_recv()
    att_pair[tokens:] = att_sib[...]

    half = planes // 2
    for d in range(half):
        reduce_2(targets[d])
    ahead = targets[half:]
    grad_acc = jnp.zeros((2 * tokens, HEADS * HEAD), F32)
    for d in sources:
        pass_diag(d)
        w = full_w[plane_before(d), :, core].reshape(4 * rows, HEADS * HEAD)
        grad_acc = grad_acc + dot(cot_sel[plane_before(d)], w, NN)
        if ahead:
            reduce_2(ahead.pop(0))
    grad_sib[...] = grad_acc[tokens:]
    start(exchanges[2])
    own_grad = grad_acc[:tokens]
    reduce_3(targets[0])
    exchanges[2].wait_recv()
    grad[...] = ((own_grad + grad_in[...]) * scale).astype(BF16)
    pieces(1, q_ref, grad)
    send_pieces(1)

    stores = []

    def put(i, src, dst):
        c = pltpu.make_async_copy(src, dst, store.at[i])
        c.start()
        stores.append(c)

    def mix(i):
        w = full_w[i].reshape(width, w_ref.shape[1])
        cols = pl.ds(i * width, width)
        mixed_ref[:, cols] = dot(att[...], w, NT).astype(BF16)
        put(4 + i, mixed_ref.at[:, cols], mixed_hbm.at[:, cols])

    for d in range(1, half):
        reduce_3(targets[d])
    reduce_4(targets[0])
    send_totals(1)
    for d in range(half, planes):
        reduce_3(targets[d])
    for h in range(HEADS):
        cols = slice(h * HEAD, (h + 1) * HEAD)
        q, k, v, g = head(q_ref, h), head(k_ref, h), head(v_ref, h), head(grad, h)
        gs = jnp.where(causal, dot(g, v, NT), 0.0).astype(BF16)
        dq_ref[:, cols] = (dot(gs, k, NN) + dot(g, state_of(0, h), NT)).astype(BF16)
        dk_part[:, cols] = dot(gs, q, TN)
        dv_part[:, cols] = dot(scores[h], g, TN)
    send_prefixes(1)
    put(0, dq_ref, dq_hbm)
    for d in range(1, half):
        reduce_4(targets[d])
    for d in range(planes):
        for i in range(4):
            sib_copy(d, i).wait_recv()
    mix(0)
    for d in range(half, planes - 1):
        reduce_4(targets[d])
    wait_state(1)
    for h in range(HEADS):
        cols = slice(h * HEAD, (h + 1) * HEAD)
        k, v = head(k_ref, h), head(v_ref, h)
        dk_ref[:, cols] = (dk_part[:, cols] + dot(v, state_of(1, h), NT)).astype(BF16)
        dv_ref[:, cols] = (dv_part[:, cols] + dot(k, state_of(1, h), NN)).astype(BF16)
    put(1, dk_ref, dk_hbm)
    put(2, dv_ref, dv_hbm)
    for i in range(1, planes):
        mix(i)
    reduce_4(0)
    reduce_5()
    put(3, wg_ref, wg_hbm)
    for c in sent:
        c.wait_send()
    for c in stores:
        c.wait()


def place(*refs):
    load, store = refs[15:]
    loads = [pltpu.make_async_copy(refs[i], refs[10 + i], load.at[i]) for i in range(5)]
    stores = [pltpu.make_async_copy(refs[10 + i], refs[5 + i], store.at[i]) for i in range(5)]
    for c in loads:
        c.start()
    for i in range(5):
        loads[i].wait()
        stores[i].start()
    for c in stores:
        c.wait()


def body(planes, queries, keys, values, out_weight, cotangent):
    tokens, hf = queries.shape
    rows = out_weight.shape[0]
    half = HEAD // 2
    dma = pltpu.SemaphoreType.DMA
    hbm = pl.BlockSpec(memory_space=pl.ANY)
    blocks = pltpu.VMEM((planes, rows, hf), BF16)
    results = pl.pallas_call(
        functools.partial(kernel, planes),
        out_shape=(
            jax.ShapeDtypeStruct(cotangent.shape, BF16),
            jax.ShapeDtypeStruct(queries.shape, BF16),
            jax.ShapeDtypeStruct(queries.shape, BF16),
            jax.ShapeDtypeStruct(queries.shape, BF16),
            jax.ShapeDtypeStruct(out_weight.shape, F32),
        ),
        in_specs=[hbm] * 5,
        out_specs=(hbm,) * 5,
        scratch_shapes=[
            pltpu.VMEM(cotangent.shape, BF16),
            pltpu.VMEM(queries.shape, BF16),
            pltpu.VMEM(queries.shape, BF16),
            pltpu.VMEM(queries.shape, BF16),
            pltpu.VMEM(out_weight.shape, F32),
            dma((4 + planes,)),
            pltpu.VMEM(queries.shape, BF16),
            pltpu.VMEM(queries.shape, BF16),
            pltpu.VMEM(queries.shape, BF16),
            pltpu.VMEM(cotangent.shape, BF16),
            pltpu.VMEM((planes, 4, 2, rows, tokens), BF16),
            dma((5,)),
            pltpu.VMEM((planes, 4, rows, tokens), BF16),
            pltpu.VMEM((planes, 2 * tokens, 4 * rows), BF16),
            pltpu.VMEM((2 * tokens, hf), BF16),
            pltpu.VMEM((tokens, hf), BF16),
            pltpu.VMEM((tokens, hf), F32),
            pltpu.VMEM((tokens, hf), F32),
            pltpu.VMEM((tokens, hf), F32),
            pltpu.VMEM((tokens, hf), F32),
            pltpu.VMEM((planes, 4, 2, rows, hf), BF16),
            pltpu.VMEM((planes, 4, rows, hf), BF16),
            blocks, blocks, blocks, blocks, blocks,
            pltpu.VMEM((rows, hf), F32),
            pltpu.VMEM((HEADS, tokens, tokens), BF16),
            pltpu.VMEM((HEADS, tokens, HEAD), F32),
            pltpu.VMEM((tokens, hf), BF16),
            pltpu.VMEM((tokens, hf), BF16),
            pltpu.VMEM((2, GROUP, half, HEAD), BF16),
            pltpu.VMEM((2, GROUP, half, HEAD), BF16),
            pltpu.VMEM((2, half, HEAD), F32),
            pltpu.VMEM((2, planes, half, HEAD), F32),
            pltpu.VMEM((2, GROUP, half, HEAD), BF16),
            pltpu.VMEM((2, GROUP, half, HEAD), BF16),
            dma((2, GROUP)), dma((2, GROUP)),
            dma((2, planes)), dma((2, planes)),
            dma((2, GROUP)), dma((2, GROUP)),
        ] + [dma((planes,))] * 8 + [dma((planes, 4))] * 2 + [dma((3,))] * 2 + [dma((planes,))] * 8,
        compiler_params=pltpu.CompilerParams(
            collective_id=0, has_side_effects=True, vmem_limit_bytes=60 * 1024 * 1024
        ),
    )(queries, keys, values, out_weight, cotangent)
    return pl.pallas_call(
        place,
        out_shape=[jax.ShapeDtypeStruct(r.shape, r.dtype) for r in results],
        in_specs=[hbm] * 5,
        out_specs=[hbm] * 5,
        scratch_shapes=[pltpu.VMEM(r.shape, r.dtype) for r in results] + [dma((5,))] * 2,
        compiler_params=pltpu.CompilerParams(vmem_limit_bytes=60 * 1024 * 1024),
    )(*results)


def solution(mesh):
    planes = mesh.shape["ctx"] // GROUP
    spec = P("ctx", None)
    return jax.shard_map(
        functools.partial(body, planes),
        mesh=mesh,
        in_specs=(spec,) * 5,
        out_specs=(spec,) * 5,
        check_vma=False,
    )
```

```python
import functools

import jax
import jax.numpy as jnp
from jax import lax
from jax.experimental import pallas as pl
from jax.experimental.pallas import tpu as pltpu
from jax.sharding import PartitionSpec as P

HEADS = 4
HEAD = 128
GROUP = 8
F32 = jnp.float32
BF16 = jnp.bfloat16
MESH = pl.DeviceIdType.MESH


def dot(x, y, dims):
    return lax.dot_general(x, y, (dims, ((), ())), preferred_element_type=F32)


NN = ((1,), (0,))
NT = ((1,), (1,))
TN = ((0,), (0,))


def kernel(
    planes,
    q_hbm, k_hbm, v_hbm, w_ref, cot_hbm,
    mixed_hbm, dq_hbm, dk_hbm, dv_hbm, wg_hbm,
    mixed_ref, dq_ref, dk_ref, dv_ref, wg_ref, store,
    q_ref, k_ref, v_ref, cot_ref, cot_t, load,
    cot_sib, cot_sel, att_pair, att_sib, grad_sib, grad_in, dk_part, dv_part,
    full_w, summed, from_diag, from_x, from_y, to_plane, from_plane, own_sum,
    scores, local_part, att, grad,
    piece_out, piece_in, total_out, totals, prefix_out, state,
    p1_send, p1_recv, p2_send, p2_recv, p3_send, p3_recv,
    z_send, z_recv, x_send, x_recv, y_send, y_recv, g_send, g_recv, s_send, s_recv,
    e_send, e_recv, rd_send, rd_recv, rx_send, rx_recv, ry_send, ry_recv, rz_send, rz_recv,
):
    tokens = q_ref.shape[0]
    rows = w_ref.shape[0]
    width = GROUP * rows
    me = lax.axis_index("ctx")
    plane = lax.div(me, GROUP)
    member = lax.rem(me, GROUP)
    core = lax.rem(member, 2)
    quad = lax.div(member, 2)
    quad_x = lax.rem(quad, 2)
    quad_y = lax.div(quad, 2)
    to_x = 1 - 2 * quad_x
    to_y = 2 - 4 * quad_y
    col_x = quad + to_x
    col_y = quad + to_y
    col_d = 3 - quad
    x_dev = me + 2 * to_x
    y_dev = me + 2 * to_y
    sib = me + 1 - 2 * core
    other = 1 - core

    def mate(r):
        return lax.rem(member + r, GROUP)

    def mate_dev(r):
        return plane * GROUP + mate(r)

    def plane_at(d):
        return lax.rem(plane + d, planes)

    def plane_before(d):
        return lax.rem(plane + planes - d, planes)

    def plane_dev(d):
        return plane_at(d) * GROUP + member

    def copy(src, dst, send, recv, device):
        return pltpu.make_async_remote_copy(
            src_ref=src, dst_ref=dst, send_sem=send, recv_sem=recv,
            device_id=(device,), device_id_type=MESH,
        )

    sent = []

    def start(c):
        c.start()
        sent.append(c)

    loads = [
        pltpu.make_async_copy(src, dst, load.at[i])
        for i, (src, dst) in enumerate((
            (k_hbm, k_ref), (v_hbm, v_ref), (q_hbm, q_ref),
            (w_ref, full_w.at[plane, quad, core]), (cot_hbm, cot_ref),
        ))
    ]
    for c in loads:
        c.start()

    barrier = pltpu.get_barrier_semaphore()
    for r in range(1, GROUP):
        pl.semaphore_signal(barrier, inc=1, device_id=(mate_dev(r),), device_id_type=MESH)
    for d in range(1, planes):
        pl.semaphore_signal(barrier, inc=1, device_id=(plane_dev(d),), device_id_type=MESH)

    def head(ref, h):
        return ref[:, h * HEAD:(h + 1) * HEAD]

    def pieces(way, left, right):
        for h in range(HEADS):
            outer = dot(head(left, h), head(right, h), TN).astype(BF16)
            piece_out[way, 2 * h:2 * h + 2] = outer.reshape(2, HEAD // 2, HEAD)

    def piece_copy(way, r):
        return copy(piece_out.at[way, mate(r)], piece_in.at[way, member],
                    p1_send.at[way, r], p1_recv.at[way, r], mate_dev(r))

    def send_pieces(way):
        for r in range(1, GROUP):
            start(piece_copy(way, r))
        piece_in[way, member] = piece_out[way, member]

    def total_copy(way, d):
        return copy(total_out.at[way], totals.at[way, plane],
                    p2_send.at[way, d], p2_recv.at[way, d], plane_dev(d))

    def send_totals(way):
        for r in range(1, GROUP):
            piece_copy(way, r).wait_recv()
        total = piece_in[way, 0].astype(F32)
        for j in range(1, GROUP):
            total = total + piece_in[way, j].astype(F32)
        total_out[way] = total
        totals[way, plane] = total
        for d in range(1, planes):
            start(total_copy(way, d))

    def prefix_copy(way, r):
        return copy(prefix_out.at[way, mate(r)], state.at[way, member],
                    p3_send.at[way, r], p3_recv.at[way, r], mate_dev(r))

    def send_prefixes(way):
        for d in range(1, planes):
            total_copy(way, d).wait_recv()
        run = jnp.zeros((HEAD // 2, HEAD), F32)
        for i in range(planes):
            counts = (i < plane) if way == 0 else (i > plane)
            run = run + jnp.where(counts, totals[way, i], 0.0)
        for j in (range(GROUP) if way == 0 else range(GROUP - 1, -1, -1)):
            prefix_out[way, j] = run.astype(BF16)
            run = run + piece_in[way, j].astype(F32)
        for r in range(1, GROUP):
            start(prefix_copy(way, r))
        state[way, member] = prefix_out[way, member]

    def wait_state(way):
        for r in range(1, GROUP):
            prefix_copy(way, r).wait_recv()

    def state_of(way, h):
        return state[way, 2 * h:2 * h + 2].reshape(HEAD, HEAD)

    def z_copy(d):
        return copy(w_ref, full_w.at[plane, quad, core], z_send.at[d], z_recv.at[d], plane_dev(d))

    def block(d, col):
        return full_w.at[plane_before(d), col, core]

    def move(d, col, sems, device, first=False):
        send, recv = sems
        return copy(w_ref if first else block(d, col), block(d, col), send, recv, device)

    def x_copy(d, first=False):
        return move(d, quad, (x_send.at[d], x_recv.at[d]), x_dev, first)

    def y_copy(d, first=False):
        return move(d, quad, (y_send.at[d], y_recv.at[d]), y_dev, first)

    def diag_copy(d):
        if d % 2 == 0:
            return move(d, col_y, (g_send.at[d], g_recv.at[d]), x_dev)
        return move(d, col_x, (g_send.at[d], g_recv.at[d]), y_dev)

    def sib_copy(d, i, first=False):
        col = (quad, col_x, col_y, col_d)[i]
        return move(d, col, (s_send.at[d, i], s_recv.at[d, i]), sib, first)

    def spread(d):
        if d:
            z_copy(d).wait_recv()
        start(x_copy(d, d == 0))
        start(y_copy(d, d == 0))
        start(sib_copy(d, 0, d == 0))

    def pass_on(d):
        x_copy(d).wait_recv()
        if d % 2:
            start(diag_copy(d))
        start(sib_copy(d, 1))
        y_copy(d).wait_recv()
        if d % 2 == 0:
            start(diag_copy(d))
        start(sib_copy(d, 2))

    def pass_diag(d):
        diag_copy(d).wait_recv()
        start(sib_copy(d, 3))

    exchanges = [
        copy(src, dst, e_send.at[i], e_recv.at[i], sib)
        for i, (src, dst) in enumerate((
            (cot_t.at[:, :, other], cot_sib), (att, att_sib), (grad_sib, grad_in),
        ))
    ]

    def rd_copy(d):
        return copy(summed.at[d, col_d], from_diag.at[d], rd_send.at[d], rd_recv.at[d],
                    y_dev if d % 2 else x_dev)

    def rx_copy(d):
        return copy(summed.at[d, col_x], from_x.at[d], rx_send.at[d], rx_recv.at[d], x_dev)

    def ry_copy(d):
        return copy(summed.at[d, col_y], from_y.at[d], ry_send.at[d], ry_recv.at[d], y_dev)

    def reduce_2(d):
        a = plane_at(d)
        tall = jnp.concatenate([cot_t[a, :, core], cot_sib[a]], axis=-1)
        term = dot(tall.reshape(4 * rows, 2 * tokens), att_pair[...], NN).astype(BF16)
        summed[d] = term.reshape(4, rows, HEADS * HEAD)
        start(rd_copy(d))
        start(ry_copy(d) if d % 2 else rx_copy(d))

    def reduce_3(d):
        rd_copy(d).wait_recv()
        col = col_x if d % 2 else col_y
        both = summed[d, col].astype(F32) + from_diag[d].astype(F32)
        summed[d, col] = both.astype(BF16)
        start(rx_copy(d) if d % 2 else ry_copy(d))

    def rz_copy(d):
        return copy(to_plane.at[d], from_plane.at[d], rz_send.at[d], rz_recv.at[d], plane_dev(d))

    def reduce_4(d):
        rx_copy(d).wait_recv()
        ry_copy(d).wait_recv()
        total = summed[d, quad].astype(F32) + from_x[d].astype(F32) + from_y[d].astype(F32)
        if d:
            to_plane[d] = total.astype(BF16)
            start(rz_copy(d))
        else:
            own_sum[...] = total

    def reduce_5():
        total = own_sum[...]
        for d in range(1, planes):
            rz_copy(d).wait_recv()
            total = total + from_plane[d].astype(F32)
        wg_ref[...] = total

    targets = list(range(2, planes)) + [1, 0]
    sources = [0, 1] + list(range(planes - 1, 1, -1))

    position = me * tokens + lax.broadcasted_iota(jnp.int32, (tokens, 1), 0)
    scale = lax.rsqrt(HEAD * (position + 1).astype(F32))
    causal = lax.broadcasted_iota(jnp.int32, (tokens, tokens), 0) >= lax.broadcasted_iota(
        jnp.int32, (tokens, tokens), 1
    )

    loads[0].wait()
    loads[1].wait()
    pieces(0, k_ref, v_ref)
    pl.semaphore_wait(barrier, GROUP - 1 + planes - 1)
    send_pieces(0)
    start(z_copy(1))
    spread(0)
    loads[2].wait()
    for h in range(HEADS):
        s = jnp.where(causal, dot(head(q_ref, h), head(k_ref, h), NT), 0.0).astype(BF16)
        scores[h] = s
        local_part[h] = dot(s, head(v_ref, h), NN)
    send_totals(0)
    for d in sources[2:]:
        start(z_copy(d))
    loads[4].wait()
    for i in range(planes):
        cot_t[i] = cot_ref[:, i * width:(i + 1) * width].T.reshape(4, 2, rows, tokens)
    start(exchanges[0])
    spread(1)
    send_prefixes(0)
    for i in range(planes):
        cot_sel[i, :tokens] = cot_t[i, :, core].reshape(4 * rows, tokens).T
    pass_on(0)
    spread(sources[2])
    loads[3].wait()
    wait_state(0)
    for h in range(HEADS):
        a = (local_part[h] + dot(head(q_ref, h), state_of(0, h), NN)) * scale
        att[:, h * HEAD:(h + 1) * HEAD] = a.astype(BF16)
    start(exchanges[1])
    pass_on(1)
    for d in sources[3:]:
        spread(d)
    att_pair[:tokens] = att[...]
    exchanges[0].wait_recv()
    for i in range(planes):
        cot_sel[i, tokens:] = cot_sib[i].reshape(4 * rows, tokens).T
    for d in sources[2:]:
        pass_on(d)
    exchanges[1].wait_recv()
    att_pair[tokens:] = att_sib[...]

    half = planes // 2
    grad_acc = jnp.zeros((2 * tokens, HEADS * HEAD), F32)
    for d in sources:
        pass_diag(d)
        w = full_w[plane_before(d), :, core].reshape(4 * rows, HEADS * HEAD)
        grad_acc = grad_acc + dot(cot_sel[plane_before(d)], w, NN)
    grad_sib[...] = grad_acc[tokens:]
    start(exchanges[2])
    own_grad = grad_acc[:tokens]
    for d in range(half):
        reduce_2(targets[d])
    exchanges[2].wait_recv()
    grad[...] = ((own_grad + grad_in[...]) * scale).astype(BF16)
    pieces(1, q_ref, grad)
    send_pieces(1)

    stores = []

    def put(i, src, dst):
        c = pltpu.make_async_copy(src, dst, store.at[i])
        c.start()
        stores.append(c)

    def mix(i):
        w = full_w[i].reshape(width, w_ref.shape[1])
        cols = pl.ds(i * width, width)
        mixed_ref[:, cols] = dot(att[...], w, NT).astype(BF16)
        put(4 + i, mixed_ref.at[:, cols], mixed_hbm.at[:, cols])

    for d in range(half):
        reduce_3(targets[d])
    send_totals(1)
    for h in range(HEADS):
        cols = slice(h * HEAD, (h + 1) * HEAD)
        q, k, v, g = head(q_ref, h), head(k_ref, h), head(v_ref, h), head(grad, h)
        gs = jnp.where(causal, dot(g, v, NT), 0.0).astype(BF16)
        dq_ref[:, cols] = (dot(gs, k, NN) + dot(g, state_of(0, h), NT)).astype(BF16)
        dk_part[:, cols] = dot(gs, q, TN)
        dv_part[:, cols] = dot(scores[h], g, TN)
    send_prefixes(1)
    for d in range(half, planes):
        reduce_2(targets[d])
    put(0, dq_ref, dq_hbm)
    for d in range(half):
        reduce_4(targets[d])
    for d in range(half, planes):
        reduce_3(targets[d])
    for d in range(planes):
        for i in range(4):
            sib_copy(d, i).wait_recv()
    mix(0)
    for d in range(half, planes - 1):
        reduce_4(targets[d])
    wait_state(1)
    for h in range(HEADS):
        cols = slice(h * HEAD, (h + 1) * HEAD)
        k, v = head(k_ref, h), head(v_ref, h)
        dk_ref[:, cols] = (dk_part[:, cols] + dot(v, state_of(1, h), NT)).astype(BF16)
        dv_ref[:, cols] = (dv_part[:, cols] + dot(k, state_of(1, h), NN)).astype(BF16)
    put(1, dk_ref, dk_hbm)
    put(2, dv_ref, dv_hbm)
    for i in range(1, planes):
        mix(i)
    reduce_4(0)
    reduce_5()
    put(3, wg_ref, wg_hbm)
    for c in sent:
        c.wait_send()
    for c in stores:
        c.wait()


def place(*refs):
    load, store = refs[15:]
    loads = [pltpu.make_async_copy(refs[i], refs[10 + i], load.at[i]) for i in range(5)]
    stores = [pltpu.make_async_copy(refs[10 + i], refs[5 + i], store.at[i]) for i in range(5)]
    for c in loads:
        c.start()
    for i in range(5):
        loads[i].wait()
        stores[i].start()
    for c in stores:
        c.wait()


def body(planes, queries, keys, values, out_weight, cotangent):
    tokens, hf = queries.shape
    rows = out_weight.shape[0]
    half = HEAD // 2
    dma = pltpu.SemaphoreType.DMA
    hbm = pl.BlockSpec(memory_space=pl.ANY)
    blocks = pltpu.VMEM((planes, rows, hf), BF16)
    results = pl.pallas_call(
        functools.partial(kernel, planes),
        out_shape=(
            jax.ShapeDtypeStruct(cotangent.shape, BF16),
            jax.ShapeDtypeStruct(queries.shape, BF16),
            jax.ShapeDtypeStruct(queries.shape, BF16),
            jax.ShapeDtypeStruct(queries.shape, BF16),
            jax.ShapeDtypeStruct(out_weight.shape, F32),
        ),
        in_specs=[hbm] * 5,
        out_specs=(hbm,) * 5,
        scratch_shapes=[
            pltpu.VMEM(cotangent.shape, BF16),
            pltpu.VMEM(queries.shape, BF16),
            pltpu.VMEM(queries.shape, BF16),
            pltpu.VMEM(queries.shape, BF16),
            pltpu.VMEM(out_weight.shape, F32),
            dma((4 + planes,)),
            pltpu.VMEM(queries.shape, BF16),
            pltpu.VMEM(queries.shape, BF16),
            pltpu.VMEM(queries.shape, BF16),
            pltpu.VMEM(cotangent.shape, BF16),
            pltpu.VMEM((planes, 4, 2, rows, tokens), BF16),
            dma((5,)),
            pltpu.VMEM((planes, 4, rows, tokens), BF16),
            pltpu.VMEM((planes, 2 * tokens, 4 * rows), BF16),
            pltpu.VMEM((2 * tokens, hf), BF16),
            pltpu.VMEM((tokens, hf), BF16),
            pltpu.VMEM((tokens, hf), F32),
            pltpu.VMEM((tokens, hf), F32),
            pltpu.VMEM((tokens, hf), F32),
            pltpu.VMEM((tokens, hf), F32),
            pltpu.VMEM((planes, 4, 2, rows, hf), BF16),
            pltpu.VMEM((planes, 4, rows, hf), BF16),
            blocks, blocks, blocks, blocks, blocks,
            pltpu.VMEM((rows, hf), F32),
            pltpu.VMEM((HEADS, tokens, tokens), BF16),
            pltpu.VMEM((HEADS, tokens, HEAD), F32),
            pltpu.VMEM((tokens, hf), BF16),
            pltpu.VMEM((tokens, hf), BF16),
            pltpu.VMEM((2, GROUP, half, HEAD), BF16),
            pltpu.VMEM((2, GROUP, half, HEAD), BF16),
            pltpu.VMEM((2, half, HEAD), F32),
            pltpu.VMEM((2, planes, half, HEAD), F32),
            pltpu.VMEM((2, GROUP, half, HEAD), BF16),
            pltpu.VMEM((2, GROUP, half, HEAD), BF16),
            dma((2, GROUP)), dma((2, GROUP)),
            dma((2, planes)), dma((2, planes)),
            dma((2, GROUP)), dma((2, GROUP)),
        ] + [dma((planes,))] * 8 + [dma((planes, 4))] * 2 + [dma((3,))] * 2 + [dma((planes,))] * 8,
        compiler_params=pltpu.CompilerParams(
            collective_id=0, has_side_effects=True, vmem_limit_bytes=60 * 1024 * 1024
        ),
    )(queries, keys, values, out_weight, cotangent)
    return pl.pallas_call(
        place,
        out_shape=[jax.ShapeDtypeStruct(r.shape, r.dtype) for r in results],
        in_specs=[hbm] * 5,
        out_specs=[hbm] * 5,
        scratch_shapes=[pltpu.VMEM(r.shape, r.dtype) for r in results] + [dma((5,))] * 2,
        compiler_params=pltpu.CompilerParams(vmem_limit_bytes=60 * 1024 * 1024),
    )(*results)


def solution(mesh):
    planes = mesh.shape["ctx"] // GROUP
    spec = P("ctx", None)
    return jax.shard_map(
        functools.partial(body, planes),
        mesh=mesh,
        in_specs=(spec,) * 5,
        out_specs=(spec,) * 5,
        check_vma=False,
    )
```
